128 devices in a mesh: seq: 16 (over z, y), head: 8 (over x, core).
Axes of the slice: x: 4, y: 4, z: 4, core: 2. Of those that a mesh axis runs over, the one named last changes fastest.
Arguments:
- latents: bfloat16 [2048, 2048], replicated, may hold values from -120 to 120
- context: bfloat16 [16384, 2048], P('seq'), may hold values from -6 to 6
- offsets: int32 [2048], replicated, may hold values from 14336 to 16383, as said below
- w_query: bfloat16 [2048, 2048], P(None, 'head'), may hold values from -1 to 1
- w_key: bfloat16 [2048, 2048], P(None, 'head'), may hold values from -1 to 1
- w_value: bfloat16 [2048, 2048], P(None, 'head'), may hold values from -0.125 to 0.125
- grad_out: bfloat16 [2048, 2048], P(None, 'head'), may hold values from -6 to 6
Outputs:
- attention_out: bfloat16 [2048, 2048], P('seq', 'head')
- grad_latents: bfloat16 [2048, 2048], P('seq', 'head')
- grad_context: bfloat16 [16384, 2048], P('seq', 'head')
The draws below stay inside these ranges and needn't reach their ends.
Inputs may be any that keep to these rules, and one draw needn't show every extreme that they name: Latent query i sees context positions 0 through offsets[i]; the latents are causal: offsets[i] = min(s + i, 16383) for one shift s of the draw, so the latents' own span ends at or runs past the stretch's last position and latents past it see the whole stretch.
All inputs are finite; a program needn't handle non-finite values.
Results may differ from the reference program's by a relative error of at most 0.028.
Values may be sent and summed in bfloat16 or wider, within the bound.
A program may use at most 128 MiB of HBM per device.

```python
import jax
import jax.numpy as jnp
from jax import lax

D = 2048
H = 16
E = 128
LAT = 2048
TOK_DEV = 1024
TOKENS = 16384
N_SEQ = 16
N_HEAD = 8


def shared_context(key):
    gauss = jnp.clip(jax.random.normal(jax.random.fold_in(key, 903), (TOKENS, D), jnp.float32), -6.0, 6.0)
    return gauss


def draw_offsets(key, part):
    key = jax.random.fold_in(key, 1)
    shift = jax.random.randint(key, (), 0, LAT // 2 + 1, jnp.int32)
    ends = TOKENS - LAT + jnp.arange(LAT, dtype=jnp.int32) + shift
    return jnp.minimum(ends, TOKENS - 1).astype(jnp.int32)


def draw_context(key, part):
    gauss = shared_context(key)
    result = gauss
    return result.astype(jnp.bfloat16)


def draw_latents(key, part):
    key = jax.random.fold_in(key, 3)
    result = 2.5 * jnp.clip(jax.random.normal(key, (LAT, D), jnp.float32), -6.0, 6.0)
    return result.astype(jnp.bfloat16)


def draw_w_query(key, part):
    key = jax.random.fold_in(key, 4)
    own = jnp.clip(jax.random.normal(key, (D, H * E), jnp.float32), -6.0, 6.0)
    result = own
    return (result * D ** (-0.5)).astype(jnp.bfloat16)


def draw_w_key(key, part):
    key = jax.random.fold_in(key, 5)
    own = jnp.clip(jax.random.normal(key, (D, H * E), jnp.float32), -6.0, 6.0)
    result = own
    return (result * D ** (-0.5)).astype(jnp.bfloat16)


def levels(rng, shape, shards, least, high):
    loudness, own = 1.0, jax.random.fold_in(rng, 6)
    for position, shards_of in shards:
        steps = jnp.exp(jax.random.uniform(jax.random.fold_in(own, position), (shards_of,), jnp.float32, least / len(shards), high / len(shards)))
        loudness = loudness * jnp.repeat(steps, shape[position] // shards_of).reshape([-1 if axis == position else 1 for axis in range(len(shape))])
    return loudness


def centred(stream_key, dims, width, bound, pieces=(), kind=jnp.bfloat16):
    values = width * jax.random.normal(stream_key, dims, jnp.float32)
    if pieces:
        values = values * levels(stream_key, dims, pieces, -0.22, 0.18)
    return jnp.clip(values, -bound, bound).astype(kind)


def setup_inputs(seed: int = 0) -> dict:
    key_list = jax.random.split(jax.random.key(seed), 8)
    return {
        "latents": draw_latents(jax.random.fold_in(key_list[7], 71), 0),
        "context": draw_context(jax.random.fold_in(key_list[7], 71), 0),
        "offsets": draw_offsets(jax.random.fold_in(key_list[7], 71), 0),
        "w_query": draw_w_query(jax.random.fold_in(key_list[7], 71), 0),
        "w_key": draw_w_key(jax.random.fold_in(key_list[7], 71), 0),
        "w_value": centred(key_list[5], (D, H * E), D ** -0.5, 0.125, ((1, 8),)),
        "grad_out": centred(key_list[6], (LAT, H * E), 1.0, 6.0, ((1, 8),)),
    }


masked_floor = -1.0e30


def reference(latents, context, offsets, w_query, w_key, w_value, grad_out):
    scaling = E ** -0.5
    query_rows = jnp.dot(latents, w_query, preferred_element_type=jnp.float32).astype(jnp.bfloat16)
    key_rows = jnp.dot(context, w_key, preferred_element_type=jnp.float32).astype(jnp.bfloat16)
    value_rows = jnp.dot(context, w_value, preferred_element_type=jnp.float32).astype(jnp.bfloat16)
    positions = jnp.arange(TOKENS, dtype=jnp.int32)
    visible = positions[None, :] <= offsets[:, None]
    blocked_visible = visible.reshape(LAT, N_SEQ, TOK_DEV)

    def split_heads(matrix, rows):
        return matrix.reshape(rows, H, E).transpose(1, 0, 2)

    def one_head(operands):
        query_head, key_head, value_head, grad_head = operands
        scores = jnp.dot(query_head, key_head.T, preferred_element_type=jnp.float32) * scaling
        blocked = scores.reshape(LAT, N_SEQ, TOK_DEV)
        block_max = jnp.max(jnp.where(blocked_visible, blocked, masked_floor), axis=2)
        block_weight = jnp.where(blocked_visible, jnp.exp(blocked - block_max[:, :, None]), 0.0)
        block_sum = jnp.sum(block_weight, axis=2)
        rounded = block_weight.astype(jnp.bfloat16).astype(jnp.float32)
        value_blocks = value_head.reshape(N_SEQ, TOK_DEV, E).astype(jnp.float32)
        block_out = jnp.einsum('inj,nje->ine', rounded, value_blocks)
        row_max = jnp.max(block_max, axis=1)
        factor = jnp.exp(block_max - row_max[:, None])
        total = jnp.sum(block_sum * factor, axis=1)
        merged = jnp.sum(block_out * factor[:, :, None], axis=1)
        attention = (merged / total[:, None]).astype(jnp.bfloat16)
        log_total = row_max + jnp.log(total)
        row_delta = jnp.sum(grad_head.astype(jnp.float32) * attention.astype(jnp.float32), axis=1)
        probabilities = jnp.where(visible, jnp.exp(scores - log_total[:, None]), 0.0)
        grad_values = jnp.dot(probabilities.astype(jnp.bfloat16).T, grad_head, preferred_element_type=jnp.float32).astype(jnp.bfloat16)
        grad_probs = jnp.dot(grad_head, value_head.T, preferred_element_type=jnp.float32)
        grad_scores = (probabilities * (grad_probs - row_delta[:, None])).astype(jnp.bfloat16)
        grad_query = jnp.dot(grad_scores, key_head, preferred_element_type=jnp.float32) * scaling
        grad_keys = (jnp.dot(grad_scores.T, query_head, preferred_element_type=jnp.float32) * scaling).astype(jnp.bfloat16)
        return attention, grad_query, grad_keys, grad_values

    results = lax.map(one_head, (split_heads(query_rows, LAT), split_heads(key_rows, TOKENS), split_heads(value_rows, TOKENS), split_heads(grad_out, LAT)))
    attention_out = results[0].transpose(1, 0, 2).reshape(LAT, H * E)
    grad_query = results[1].transpose(1, 0, 2).reshape(LAT, H * E).astype(jnp.bfloat16)
    grad_keys = results[2].transpose(1, 0, 2).reshape(TOKENS, H * E)
    grad_values = results[3].transpose(1, 0, 2).reshape(TOKENS, H * E)
    grad_latents = jnp.dot(grad_query, w_query.T, preferred_element_type=jnp.float32).astype(jnp.bfloat16)
    group_width = H * E // N_HEAD
    grad_context = jnp.zeros((TOKENS, D), jnp.float32)
    for group in range(N_HEAD):
        low = group * group_width
        high = low + group_width
        group_term = jnp.dot(grad_keys[:, low:high], w_key[:, low:high].T, preferred_element_type=jnp.float32)
        group_term = group_term + jnp.dot(grad_values[:, low:high], w_value[:, low:high].T, preferred_element_type=jnp.float32)
        grad_context = grad_context + lax.optimization_barrier(group_term.astype(jnp.bfloat16)).astype(jnp.float32)
    return attention_out, grad_latents, grad_context.astype(jnp.bfloat16)
```

```python
import functools
import math

import jax
import jax.numpy as jnp
from jax import lax
from jax.experimental import pallas as pl
from jax.experimental.pallas import tpu as pltpu
from jax.sharding import PartitionSpec as P

E = 128
SCALE = E ** (-0.5)
TO_LOG2 = SCALE * math.log2(math.e)
FLOOR = -1e30
N_SEQ = 16
N_X = 4
LAT = 2048
TOK = 1024
COLS = 256
WIDE = 2048
PAIR = 256
N_PAIR = LAT // PAIR
CHUNK = 256
N_CHUNK = TOK // CHUNK
MESH = pl.DeviceIdType.MESH
BF = jnp.bfloat16
F32 = jnp.float32

NT = (((1,), (1,)), ((), ()))


def dot(a, b):
    return jnp.dot(a, b, preferred_element_type=F32)


def dot_nt(a, b):
    return lax.dot_general(a, b, NT, preferred_element_type=F32)


def kernel(
    lat_hbm, ctx_hbm, off_ref, wq_hbm, wk_hbm, wv_hbm, go_hbm,
    att_ref, gl_ref, gc_ref,
    lat, ctx, wq, wk, wv, go,
    goT, k_s, v_s, kT, vT, qT, wT,
    sflat, sbuf, srecv, obuf, orecv, res, resrecv, rows,
    gosT, fqT, dqT, dqbuf, dqrecv, dkv,
    ctxb, sibrecv, sums, arecv, bsend, brecv,
    ltb, lsib, lsums, larecv, lbsend, lbrecv,
    in_sem, st_s, st_r, o_s, o_r, rs_s, rs_r, dq_s, dq_r, sib_s, sib_r, a_s, a_r, b_s, b_r,
):
    seq = lax.axis_index("seq")
    head = lax.axis_index("head")
    core = lax.rem(head, 2)
    x = head // 2
    x_right, x_left = lax.rem(x + 1, N_X), lax.rem(x + 3, N_X)
    x_far = lax.rem(x + 2, N_X)
    sibling = x * 2 + 1 - core
    right, left = x_right * 2 + core, x_left * 2 + core

    def peer(k):
        return lax.rem(seq + k, N_SEQ)

    def load(src, dst, n):
        return pltpu.make_async_copy(src, dst, in_sem.at[n])

    def load_pair(t):
        p = lax.rem(seq // 2 + t, N_PAIR)
        return pltpu.make_async_copy(lat_hbm.at[pl.ds(p * PAIR, PAIR)], lat.at[t], in_sem.at[8 + t])

    load(wk_hbm, wk, 0).start()
    for c in range(N_CHUNK):
        rows_c = pl.ds(c * CHUNK, CHUNK)
        load(ctx_hbm.at[rows_c], ctx.at[rows_c], 4 + c).start()
        if c == 0:
            load(wv_hbm, wv, 1).start()
    load(go_hbm, go, 3).start()
    load(wq_hbm, wq, 2).start()
    for t in range(N_PAIR):
        load_pair(t).start()

    barrier = pltpu.get_barrier_semaphore()
    for k in range(1, N_SEQ):
        pl.semaphore_signal(barrier, inc=1, device_id=(peer(k), head), device_id_type=MESH)
    for h in (sibling, right, left):
        pl.semaphore_signal(barrier, inc=1, device_id=(seq, h), device_id_type=MESH)
    pl.semaphore_wait(barrier, N_SEQ - 1 + 3)

    load(wk_hbm, wk, 0).wait()
    for c in range(N_CHUNK):
        rows_c = pl.ds(c * CHUNK, CHUNK)
        load(ctx_hbm.at[rows_c], ctx.at[rows_c], 4 + c).wait()
        if c == 0:
            load(wv_hbm, wv, 1).wait()
        block = ctx[rows_c, :]
        kb = dot(block, wk[...]).astype(BF)
        k_s[rows_c, :] = kb
        kT[:, rows_c] = kb.T
        vb = dot(block, wv[...]).astype(BF)
        v_s[rows_c, :] = vb
        vT[:, rows_c] = vb.T
    load(go_hbm, go, 3).wait()

    def turn(p, _):
        at = pl.ds(pl.multiple_of(p * PAIR, PAIR), PAIR)
        goT[:, at] = go[at, :].T
        return 0

    lax.fori_loop(0, N_PAIR, turn, 0)
    load(wq_hbm, wq, 2).wait()

    def stat_copy(h, b, k):
        return pltpu.make_async_remote_copy(
            src_ref=sbuf.at[h, b], dst_ref=srecv.at[h, k], send_sem=st_s.at[h, k], recv_sem=st_r.at[h, k],
            device_id=(b, head), device_id_type=MESH)

    def out_copy(h, b, k):
        return pltpu.make_async_remote_copy(
            src_ref=obuf.at[h, b], dst_ref=orecv.at[h, k], send_sem=o_s.at[h, k], recv_sem=o_r.at[h, k],
            device_id=(b, head), device_id_type=MESH)

    def res_copy(h, k):
        return pltpu.make_async_remote_copy(
            src_ref=res.at[h], dst_ref=resrecv.at[h, seq], send_sem=rs_s.at[h, k], recv_sem=rs_r.at[h, k],
            device_id=(peer(k), head), device_id_type=MESH)

    def res_wait(h, k):
        other = lax.rem(seq + N_SEQ - k, N_SEQ)
        return pltpu.make_async_remote_copy(
            src_ref=res.at[h], dst_ref=resrecv.at[h, other], send_sem=rs_s.at[h, k], recv_sem=rs_r.at[h, k],
            device_id=(peer(k), head), device_id_type=MESH)

    def dq_copy(h, k):
        return pltpu.make_async_remote_copy(
            src_ref=dqbuf.at[h, peer(k)], dst_ref=dqrecv.at[h, k], send_sem=dq_s.at[h, k], recv_sem=dq_r.at[h, k],
            device_id=(peer(k), head), device_id_type=MESH)

    def forward(h, t):
        p = lax.rem(seq // 2 + t, N_PAIR)
        at = pl.ds(pl.multiple_of(p * PAIR, PAIR), PAIR)
        hs = slice(h * E, (h + 1) * E)
        if h == 0:
            pltpu.make_async_copy(lat_hbm.at[pl.ds(p * PAIR, PAIR)], lat.at[t], in_sem.at[8 + t]).wait()
            qT[:, at] = dot(lat[t], wq[...]).astype(BF).T
        s = dot(k_s[:, hs], qT[hs, at]) * TO_LOG2
        bound = off_ref[p] - seq * TOK
        s = jnp.where(lax.broadcasted_iota(jnp.int32, (TOK, PAIR), 0) <= bound, s, FLOOR)
        m = jnp.max(s, axis=0, keepdims=True)
        w = jnp.exp2(s - m)
        total = jnp.sum(w, axis=0, keepdims=True)
        wb = w.astype(BF)
        wT[h, :, at] = wb
        o = dot(vT[hs, :], wb)
        d = jnp.sum(goT[hs, at].astype(F32) * o, axis=0, keepdims=True)
        st = jnp.concatenate([m, total, d, jnp.zeros((5, PAIR), F32)], axis=0)
        sflat[h, :, at] = st
        ob = o.astype(BF)
        for half in range(2):
            b = 2 * p + half
            part = slice(half * 128, (half + 1) * 128)
            sbuf[h, b] = st[:, part]
            obuf[h, b] = ob[:, part]
            k = lax.rem(b - seq + N_SEQ, N_SEQ)

            @pl.when(b != seq)
            def _():
                stat_copy(h, b, k).start()
                out_copy(h, b, k).start()

    def combine(h):
        for k in range(1, N_SEQ):
            stat_copy(h, peer(k), k).wait_recv()
        own = sbuf[h, seq]
        everyone = [own] + [srecv[h, k] for k in range(1, N_SEQ)]
        top = functools.reduce(jnp.maximum, [e[0:1] for e in everyone])
        factors = [jnp.exp2(e[0:1] - top) for e in everyone]
        total = sum(e[1:2] * f for e, f in zip(everyone, factors))
        d = sum(e[2:3] * f for e, f in zip(everyone, factors)) / total
        lse = top + jnp.log2(total)
        both = jnp.concatenate([lse, d, jnp.zeros((6, 128), F32)], axis=0)
        res[h] = both
        resrecv[h, seq] = both
        for k in range(1, N_SEQ):
            res_copy(h, k).start()
        for k in range(N_SEQ):
            rows[h, k] = jnp.broadcast_to(factors[k] / total, (8, 128))

    def answers(h):
        hs = slice(h * E, (h + 1) * E)
        for k in range(1, N_SEQ):
            res_wait(h, k).wait_recv()
        lse = jnp.concatenate([resrecv[h, b, 0:1, :] for b in range(N_SEQ)], axis=1)
        delta = jnp.concatenate([resrecv[h, b, 1:2, :] for b in range(N_SEQ)], axis=1)
        f = jnp.exp2(sflat[h, 0:1, :] - lse)
        gosT[...] = (goT[hs, :].astype(F32) * f).astype(BF)
        fqT[...] = (qT[hs, :].astype(F32) * f).astype(BF)
        sflat[h, 3:4, :] = delta
        sflat[h, 4:5, :] = f * SCALE

    def backward(h, c):
        hs = slice(h * E, (h + 1) * E)
        rc = pl.ds(pl.multiple_of(c * CHUNK, CHUNK), CHUNK)
        w = wT[h, rc, :]
        dp = dot(v_s[rc, hs], goT[hs, :])
        ds = (w.astype(F32) * (dp - sflat[h, 3:4, :])).astype(BF)
        dkv[rc, h * E : (h + 1) * E] = (dot_nt(ds, fqT[...]) * SCALE).astype(BF)
        dkv[rc, COLS + h * E : COLS + (h + 1) * E] = dot_nt(w, gosT[...]).astype(BF)
        dqT[...] += dot(kT[hs, rc], ds)

    def send_query(h):
        for b in range(N_SEQ):
            at = slice(b * 128, (b + 1) * 128)
            dqbuf[h, b] = (dqT[:, at] * sflat[h, 4:5, at]).astype(BF)
        for k in range(1, N_SEQ):
            dq_copy(h, k).start()

    class Reduce:
        def __init__(self, n, term, sib, total, a_in, b_out, b_in, half):
            self.n, self.term, self.sib, self.total = n, term, sib, total
            self.a_in, self.b_out, self.b_in, self.half = a_in, b_out, b_in, half

        def to(self, src, dst, ss, rs, h):
            return pltpu.make_async_remote_copy(
                src_ref=src, dst_ref=dst, send_sem=ss, recv_sem=rs, device_id=(seq, h), device_id_type=MESH)

        def c_sib(self):
            return self.to(self.term.at[1 - core], self.sib, sib_s.at[self.n], sib_r.at[self.n], sibling)

        def c_a(self, way):
            part = pl.ds(way * self.half, self.half)
            return self.to(self.total.at[x_far, part], self.a_in.at[way], a_s.at[self.n, way], a_r.at[self.n, way],
                           (right, left)[way])

        def c_b(self, way):
            return self.to(self.b_out.at[way], self.b_in.at[way], b_s.at[self.n, way], b_r.at[self.n, way],
                           (right, left)[way])

        def step_sib(self):
            self.c_sib().start()

        def step_a(self):
            self.c_sib().wait_recv()
            for j in range(N_X):
                self.total[j] = (self.term[core, j].astype(F32) + self.sib[j].astype(F32)).astype(BF)
            for way in range(2):
                self.c_a(way).start()

        def step_b(self):
            for way in range(2):
                self.c_a(way).wait_recv()
                to = (x_right, x_left)[way]
                mine, other = pl.ds(way * self.half, self.half), pl.ds((1 - way) * self.half, self.half)
                self.b_out[way, mine, :] = (
                    self.total[to, mine, :].astype(F32) + self.a_in[way].astype(F32)).astype(BF)
                self.b_out[way, other, :] = self.total[to, other, :]
                self.c_b(way).start()

        def finish(self):
            for way in range(2):
                self.c_b(way).wait_recv()
            return (self.total[x].astype(F32) + self.b_in[0].astype(F32) + self.b_in[1].astype(F32)).astype(BF)

        def drain(self):
            self.c_sib().wait_send()
            for way in range(2):
                self.c_a(way).wait_send()
                self.c_b(way).wait_send()

    parts = [
        Reduce(c, ctxb.at[c], sibrecv.at[c], sums.at[c], arecv.at[c], bsend.at[c], brecv.at[c], CHUNK // 2)
        for c in range(N_CHUNK)
    ]
    latent_part = Reduce(N_CHUNK, ltb, lsib, lsums, larecv, lbsend, lbrecv, 64)

    def loop(n, f):
        def step(i, _):
            f(i)
            return 0

        lax.fori_loop(0, n, step, 0)

    loop(N_PAIR, lambda t: forward(0, t))
    loop(N_PAIR // 2, lambda t: forward(1, t))
    combine(0)
    loop(N_PAIR // 2, lambda t: forward(1, t + N_PAIR // 2))
    answers(0)
    dqT[...] = jnp.zeros_like(dqT)
    loop(N_CHUNK // 2, lambda c: backward(0, c))
    combine(1)
    loop(N_CHUNK // 2, lambda c: backward(0, c + N_CHUNK // 2))
    send_query(0)
    answers(1)
    dqT[...] = jnp.zeros_like(dqT)

    def context_term(c):
        rc = pl.ds(c * CHUNK, CHUNK)
        for n in range(8):
            at = slice(n * COLS, (n + 1) * COLS)
            term = dot_nt(dkv[rc, 0:COLS], wk[at, :]) + dot_nt(dkv[rc, COLS:], wv[at, :])
            ctxb[c, n % 2, n // 2] = term.astype(BF)

    for c in range(N_CHUNK):
        backward(1, c)
        if c == N_CHUNK - 1:
            send_query(1)
        context_term(c)
        parts[c].step_sib()
        if c >= 1:
            parts[c - 1].step_a()
        if c >= 2:
            parts[c - 2].step_b()
    parts[N_CHUNK - 1].step_a()
    parts[N_CHUNK - 2].step_b()

    for h in range(2):
        for k in range(1, N_SEQ):
            dq_copy(h, k).wait_recv()
    dq = jnp.concatenate(
        [
            dqbuf[h, seq].astype(F32) + sum(dqrecv[h, k].astype(F32) for k in range(1, N_SEQ))
            for h in range(2)
        ],
        axis=0,
    ).astype(BF).T
    for n in range(8):
        ltb[n % 2, n // 2] = dot_nt(dq, wq[n * COLS : (n + 1) * COLS, :]).astype(BF)
    latent_part.step_sib()
    parts[N_CHUNK - 1].step_b()
    latent_part.step_a()

    for h in range(2):
        for k in range(1, N_SEQ):
            out_copy(h, peer(k), k).wait_recv()
        o = obuf[h, seq].astype(F32) * rows[h, 0, 0:1, :]
        for k in range(1, N_SEQ):
            o = o + orecv[h, k].astype(F32) * rows[h, k, 0:1, :]
        att_ref[:, h * E : (h + 1) * E] = o.T.astype(BF)
    latent_part.step_b()
    for c in range(N_CHUNK):
        gc_ref[c * CHUNK : (c + 1) * CHUNK, :] = parts[c].finish()
    gl_ref[...] = latent_part.finish()

    for h in range(2):
        for k in range(1, N_SEQ):
            stat_copy(h, peer(k), k).wait_send()
            out_copy(h, peer(k), k).wait_send()
            res_copy(h, k).wait_send()
            dq_copy(h, k).wait_send()
    for part in [*parts, latent_part]:
        part.drain()


def body(latents, context, offsets, w_query, w_key, w_value, grad_out):
    hbm = pl.BlockSpec(memory_space=pl.ANY)
    vmem = pl.BlockSpec(memory_space=pltpu.VMEM)
    v, dma = pltpu.VMEM, pltpu.SemaphoreType.DMA
    return pl.pallas_call(
        kernel,
        out_shape=(
            jax.ShapeDtypeStruct((LAT // N_SEQ, COLS), BF),
            jax.ShapeDtypeStruct((LAT // N_SEQ, COLS), BF),
            jax.ShapeDtypeStruct((TOK, COLS), BF),
        ),
        in_specs=[hbm, hbm, vmem, hbm, hbm, hbm, hbm],
        out_specs=(vmem, vmem, vmem),
        scratch_shapes=[
            v((N_PAIR, PAIR, WIDE), BF),
            v((TOK, WIDE), BF),
            v((WIDE, COLS), BF),
            v((WIDE, COLS), BF),
            v((WIDE, COLS), BF),
            v((LAT, COLS), BF),
            v((COLS, LAT), BF),
            v((TOK, COLS), BF),
            v((TOK, COLS), BF),
            v((COLS, TOK), BF),
            v((COLS, TOK), BF),
            v((COLS, LAT), BF),
            v((2, TOK, LAT), BF),
            v((2, 8, LAT), F32),
            v((2, N_SEQ, 8, 128), F32),
            v((2, N_SEQ, 8, 128), F32),
            v((2, N_SEQ, 128, 128), BF),
            v((2, N_SEQ, 128, 128), BF),
            v((2, 8, 128), F32),
            v((2, N_SEQ, 8, 128), F32),
            v((2, N_SEQ, 8, 128), F32),
            v((E, LAT), BF),
            v((E, LAT), BF),
            v((E, LAT), F32),
            v((2, N_SEQ, 128, 128), BF),
            v((2, N_SEQ, 128, 128), BF),
            v((TOK, 2 * COLS), BF),
            v((N_CHUNK, 2, N_X, CHUNK, COLS), BF),
            v((N_CHUNK, N_X, CHUNK, COLS), BF),
            v((N_CHUNK, N_X, CHUNK, COLS), BF),
            v((N_CHUNK, 2, CHUNK // 2, COLS), BF),
            v((N_CHUNK, 2, CHUNK, COLS), BF),
            v((N_CHUNK, 2, CHUNK, COLS), BF),
            v((2, N_X, 128, COLS), BF),
            v((N_X, 128, COLS), BF),
            v((N_X, 128, COLS), BF),
            v((2, 64, COLS), BF),
            v((2, 128, COLS), BF),
            v((2, 128, COLS), BF),
            dma((16,)),
            *[dma((2, N_SEQ))] * 8,
            dma((N_CHUNK + 1,)),
            dma((N_CHUNK + 1,)),
            *[dma((N_CHUNK + 1, 2))] * 4,
        ],
        compiler_params=pltpu.CompilerParams(
            collective_id=0, has_side_effects=True, vmem_limit_bytes=60 * 1024 * 1024
        ),
        cost_estimate=pl.CostEstimate(flops=13_000_000_000, bytes_accessed=20_000_000, transcendentals=4_200_000),
    )(latents, context, offsets.reshape(N_PAIR, 1, PAIR), w_query, w_key, w_value, grad_out)


def solution(mesh):
    placed = (
        P(),
        P("seq", None),
        P(),
        P(None, "head"),
        P(None, "head"),
        P(None, "head"),
        P(None, "head"),
    )
    return jax.shard_map(
        body,
        mesh=mesh,
        in_specs=placed,
        out_specs=(P("seq", "head"), P("seq", "head"), P("seq", "head")),
        check_vma=False,
    )
```

```python
import functools
import math

import jax
import jax.numpy as jnp
from jax import lax
from jax.experimental import pallas as pl
from jax.experimental.pallas import tpu as pltpu
from jax.sharding import PartitionSpec as P

E = 128
SCALE = E ** (-0.5)
TO_LOG2 = SCALE * math.log2(math.e)
FLOOR = -1e30
N_SEQ = 16
LAT = 2048
TOK = 1024
COLS = 256
WIDE = 2048
PAIR = 256
N_PAIR = LAT // PAIR
CHUNK = 256
N_CHUNK = TOK // CHUNK
RINGS = 2
MESH = pl.DeviceIdType.MESH
BF = jnp.bfloat16
F32 = jnp.float32

NT = (((1,), (1,)), ((), ()))


def dot(a, b):
    return jnp.dot(a, b, preferred_element_type=F32)


def dot_nt(a, b):
    return lax.dot_general(a, b, NT, preferred_element_type=F32)


class Ring:
    def __init__(self, n, sems, where, ends, total, a_in, b_out, b_in, half):
        self.n, self.sems, self.half = n, sems, half
        self.me, self.right, self.left, self.far = where
        self.ends = ends
        self.total, self.a_in, self.b_out, self.b_in = total, a_in, b_out, b_in

    def copy(self, src, dst, s, r, way):
        return pltpu.make_async_remote_copy(
            src_ref=src, dst_ref=dst, send_sem=s.at[self.n, way], recv_sem=r.at[self.n, way],
            device_id=self.ends[way], device_id_type=MESH)

    def c_a(self, way):
        part = pl.ds(way * self.half, self.half)
        return self.copy(self.total.at[self.far, part], self.a_in.at[way], self.sems[0], self.sems[1], way)

    def c_b(self, way):
        return self.copy(self.b_out.at[way], self.b_in.at[way], self.sems[2], self.sems[3], way)

    def step_a(self):
        for way in range(2):
            self.c_a(way).start()

    def step_b(self):
        for way in range(2):
            self.c_a(way).wait_recv()
            to = (self.right, self.left)[way]
            mine, other = pl.ds(way * self.half, self.half), pl.ds((1 - way) * self.half, self.half)
            self.b_out[way, mine, :] = (self.total[to, mine, :].astype(F32) + self.a_in[way].astype(F32)).astype(BF)
            self.b_out[way, other, :] = self.total[to, other, :]
            self.c_b(way).start()

    def finish(self):
        for way in range(2):
            self.c_b(way).wait_recv()
        return self.total[self.me].astype(F32) + self.b_in[0].astype(F32) + self.b_in[1].astype(F32)

    def drain(self):
        for way in range(2):
            self.c_a(way).wait_send()
            self.c_b(way).wait_send()


def kernel(
    lat_hbm, ctx_hbm, off_hbm, wq_hbm, wk_hbm, wv_hbm, go_hbm,
    att_out, gl_out, gc_out,
    att_ref, gl_ref, gc_ref,
    off_ref, lat, wq, wkv, go,
    goT, k_s, v_s, kT, v1T, qT, wT, sc, mrow,
    mflat, fflat, sbuf, srecv, obuf,
    gosT, fqT, dqT, dkv, tot1, r1, tot2, r2,
    ctxb, sibrecv, arecv, bsend, brecv, xrecv,
    ltb, lsib, lrecv,
    in_sem, st_s, st_r, f_s, f_r, sib_s, sib_r, a_s, a_r, b_s, b_r, x_s, x_r, out_sem,
):
    seq = lax.axis_index("seq")
    head = lax.axis_index("head")
    core, x = lax.rem(head, 2), head // 2
    y, z = lax.rem(seq, 4), seq // 4
    ring_sems = (a_s, a_r, b_s, b_r)
    on_x, on_y, on_z = ([lax.rem(at + i, 4) for i in (0, 1, 3, 2)] for at in (x, y, z))
    x_ends = [(seq, i * 2 + core) for i in on_x[1:]]
    y_ends = [(z * 4 + i, head) for i in on_y[1:]]
    z_ends = [(i * 4 + y, head) for i in on_z[1:]]
    sibling = (seq, x * 2 + 1 - core)

    def peer(k):
        return lax.rem(seq + k, N_SEQ)

    def remote(src, dst, ss, rs, to):
        return pltpu.make_async_remote_copy(
            src_ref=src, dst_ref=dst, send_sem=ss, recv_sem=rs, device_id=to, device_id_type=MESH)

    def load(src, dst, n):
        return pltpu.make_async_copy(src, dst, in_sem.at[n])

    def load_context(c):
        rc = pl.ds(c * CHUNK, CHUNK)
        return load(ctx_hbm.at[rc], wT.at[0, rc], 4 + c)

    def load_pair(p):
        return load(lat_hbm.at[pl.ds(p * PAIR, PAIR)], lat.at[p], 8 + p)

    load_k = load(wk_hbm, wkv.at[:, pl.ds(0, COLS)], 0)
    load_v = load(wv_hbm, wkv.at[:, pl.ds(COLS, COLS)], 1)
    load_q = load(wq_hbm, wq, 2)
    load_g = load(go_hbm, go, 3)
    load_offsets = load(off_hbm, off_ref, 16)
    load_k.start()
    load_v.start()
    for c in range(N_CHUNK):
        load_context(c).start()

    barrier = pltpu.get_barrier_semaphore()
    for k in range(1, N_SEQ):
        pl.semaphore_signal(barrier, inc=1, device_id=(peer(k), head), device_id_type=MESH)
    for end in [sibling, *x_ends]:
        pl.semaphore_signal(barrier, inc=1, device_id=end, device_id_type=MESH)

    v1T[:, E:, :] = jnp.ones((2, 16, TOK), BF)
    load_k.wait()
    load_v.wait()
    for c in range(N_CHUNK):
        rc = pl.ds(c * CHUNK, CHUNK)
        load_context(c).wait()
        if c == 0:
            load_q.start()
            load_g.start()
            load_offsets.start()
            load_pair(0).start()
            load_pair(1).start()
        else:
            load_pair(2 * c).start()
            load_pair(2 * c + 1).start()
        both = dot(wT[0, rc, :], wkv[...]).astype(BF)
        kb, vb = both[:, :COLS], both[:, COLS:]
        k_s[rc, :] = kb
        kT[:, rc] = kb.T
        v_s[rc, :] = vb
        vt = vb.T
        for h in range(2):
            v1T[h, 0:E, rc] = vt[h * E : (h + 1) * E, :]
    load_g.wait()

    def lanes(p):
        return pl.ds(pl.multiple_of(p * PAIR, PAIR), PAIR)

    def turn(p, _):
        goT[:, lanes(p)] = go[lanes(p), :].T
        return 0

    lax.fori_loop(0, N_PAIR, turn, 0)
    load_q.wait()
    load_offsets.wait()

    def query(p, acc, n):
        kc = slice(n * 512, (n + 1) * 512)
        return acc + dot(lat[p, :, kc], wq[kc, :])

    def scores(p, h, j, top):
        at = lanes(p)
        hs = slice(h * E, (h + 1) * E)
        s = dot(k_s[j : j + CHUNK, hs], qT[hs, at])
        bound = off_ref[p] - (seq * TOK + j)
        s = jnp.where(lax.broadcasted_iota(jnp.int32, (CHUNK, PAIR), 0) <= bound, s, FLOOR)
        sc[h, j : j + CHUNK, :] = s
        m = jnp.max(s, axis=0, keepdims=True)
        return m if top is None else jnp.maximum(top, m)

    def stat_copy(p, k):
        return remote(sbuf.at[p], srecv.at[p, k], st_s.at[0], st_r.at[p], (peer(k), head))

    def wait_bytes(ref, sem):
        pltpu.make_async_copy(ref, ref, sem).wait()

    def forward(p, ahead, further):
        at = lanes(p)
        top = [mrow[h, 0:1, :] * TO_LOG2 for h in range(2)]
        out, then, acc = [0.0, 0.0], [None, None], 0.0
        if further:
            load_pair(p + 2).wait()
        for n in range(N_CHUNK):
            j = n * CHUNK
            for h in range(2):
                w = jnp.exp2(sc[h, j : j + CHUNK, :] * TO_LOG2 - top[h]).astype(BF)
                wT[h, j : j + CHUNK, at] = w
                out[h] = out[h] + dot(v1T[h, :, j : j + CHUNK], w)
                if ahead:
                    then[h] = scores(p + 1, h, j, then[h])
            if further:
                acc = query(p + 2, acc, n)
        if further:
            qT[:, lanes(p + 2)] = acc.astype(BF).T
        lse, delta = [], []
        for h in range(2):
            hs = slice(h * E, (h + 1) * E)
            total = out[h][E : E + 1]
            o = out[h][:E] / total
            d = jnp.sum(goT[hs, at].astype(F32) * o, axis=0, keepdims=True)
            mflat[h, :, at] = jnp.broadcast_to(top[h], (8, PAIR))
            if ahead:
                mrow[h] = jnp.broadcast_to(then[h], (8, PAIR))
            both = top[h] + jnp.log2(total)
            lse += [both[:, :128], both[:, 128:]]
            delta += [d[:, :128], d[:, 128:]]
            ob = o.astype(BF)
            for half in range(2):
                obuf[2 * p + half, hs, :] = ob[:, half * 128 : (half + 1) * 128]
        sbuf[p] = jnp.concatenate(lse + delta, axis=0)
        for k in range(1, N_SEQ):
            stat_copy(p, k).start()

    def merge(p):
        wait_bytes(srecv.at[p, pl.ds(1, N_SEQ - 1)], st_r.at[p])
        everyone = [sbuf[p]] + [srecv[p, k] for k in range(1, N_SEQ)]
        top = functools.reduce(jnp.maximum, [e[0:4] for e in everyone])
        factors = [jnp.exp2(e[0:4] - top) for e in everyone]
        total = sum(factors)
        delta = sum(e[4:8] * f for e, f in zip(everyone, factors)) / total
        lse = top + jnp.log2(total)
        share = factors[0] / total
        at = slice(p * PAIR, (p + 1) * PAIR)
        for h in range(2):
            hs = slice(h * E, (h + 1) * E)
            rows = [jnp.concatenate([a[2 * h : 2 * h + 1], a[2 * h + 1 : 2 * h + 2]], axis=1) for a in (lse, delta, share)]
            f = jnp.exp2(mflat[h, 0:1, at] - rows[0])
            fflat[h, 0:1, at] = f
            fflat[h, 1:2, at] = rows[1]
            fflat[h, 2:3, at] = rows[2]
            gosT[hs, at] = (goT[hs, at].astype(F32) * f).astype(BF)
            fqT[hs, at] = (qT[hs, at].astype(F32) * f).astype(BF)

    def grad_scores(h, c):
        hs = slice(h * E, (h + 1) * E)
        rc = pl.ds(c * CHUNK, CHUNK)
        dp = dot(v_s[rc, hs], goT[hs, :])
        ds = (wT[h, rc, :].astype(F32) * (dp - fflat[h, 1:2, :])).astype(BF)
        lat[h * N_CHUNK + c] = ds
        dq = dot(kT[hs, rc], ds)
        dqT[hs, :] = dq if c == 0 else dqT[hs, :] + dq

    class Blocks:
        def __init__(self, i):
            self.i = i
            self.axes = ((on_y, y_ends), (on_z, z_ends))

        def copies(self, h, stage):
            on, ends = self.axes[h ^ stage]
            src, dst = ((tot1, r1), (tot2, r2))[stage]
            n = 4 * self.i + 2 * h + stage
            return [
                remote(src.at[self.i, h, on[d + 1]], dst.at[self.i, h, d], f_s.at[n], f_r.at[n], ends[d]) for d in range(3)
            ]

        def start(self, h, block):
            for b in range(N_SEQ):
                to, row = (b % 4, b // 4) if h == 0 else (b // 4, b % 4)
                tot1[self.i, h, to, row * 128 : (row + 1) * 128, :] = block(h, b).astype(BF)
            for copy in self.copies(h, 0):
                copy.start()

        def total(self, h, stage):
            src, dst = ((tot1, r1), (tot2, r2))[stage]
            wait_bytes(dst.at[self.i, h], f_r.at[4 * self.i + 2 * h + stage])
            me = self.axes[h ^ stage][0][0]
            return src[self.i, h, me].astype(F32) + sum(dst[self.i, h, d].astype(F32) for d in range(3))

        def second(self, h):
            got = self.total(h, 0).astype(BF)
            for j in range(4):
                tot2[self.i, h, j] = got[j * 128 : (j + 1) * 128, :]
            for copy in self.copies(h, 1):
                copy.start()

        def finish(self, h):
            return self.total(h, 1)

        def drain(self):
            for h in range(2):
                wait_bytes(r1.at[self.i, h], f_s.at[4 * self.i + 2 * h])
                wait_bytes(r2.at[self.i, h], f_s.at[4 * self.i + 2 * h + 1])

    outs, queries = Blocks(0), Blocks(1)

    def out_block(h, b):
        at = slice(b * 128, (b + 1) * 128)
        return obuf[b, h * E : (h + 1) * E, :].astype(F32) * fflat[h, 2:3, at]

    def query_block(h, b):
        at = slice(b * 128, (b + 1) * 128)
        return dqT[h * E : (h + 1) * E, at] * (fflat[h, 0:1, at] * SCALE)

    def grad_keys_values(h, c):
        rc = pl.ds(c * CHUNK, CHUNK)
        hs = slice(h * E, (h + 1) * E)
        dkv[rc, hs] = (dot_nt(lat[h * N_CHUNK + c], fqT[hs, :]) * SCALE).astype(BF)
        dkv[rc, COLS + h * E : COLS + (h + 1) * E] = dot_nt(wT[h, rc, :], gosT[hs, :]).astype(BF)

    def context_term(c):
        rc = pl.ds(c * CHUNK, CHUNK)
        for n in range(8):
            ctxb[c, n % 2, n // 2] = dot_nt(dkv[rc, :], wkv[n * COLS : (n + 1) * COLS, :]).astype(BF)
        parts[c].sib_start()

    class Heads:
        def __init__(self, n, term, sib, ring, direct):
            self.n, self.sib, self.total = n, sib, term.at[core]
            self.c_sib = remote(term.at[1 - core], sib, sib_s.at[n], sib_r.at[n], sibling)
            self.ring = Ring(n, ring_sems, on_x, x_ends, self.total, *ring) if ring else None
            self.direct = direct

        def copies(self):
            m = self.n - RINGS
            return [remote(self.total.at[on_x[d + 1]], self.direct.at[d], x_s.at[m], x_r.at[m], x_ends[d]) for d in range(3)]

        def sib_start(self):
            self.c_sib.start()

        def a(self):
            self.c_sib.wait_recv()
            for j in range(4):
                self.total[j] = (self.total[j].astype(F32) + self.sib[j].astype(F32)).astype(BF)
            if self.ring:
                self.ring.step_a()
            else:
                for copy in self.copies():
                    copy.start()

        def b(self):
            self.ring.step_b()

        def finish(self):
            if self.ring:
                return self.ring.finish()
            wait_bytes(self.direct, x_r.at[self.n - RINGS])
            return self.total[x].astype(F32) + sum(self.direct[d].astype(F32) for d in range(3))

        def drain(self):
            self.c_sib.wait_send()
            if self.ring:
                self.ring.drain()
            else:
                wait_bytes(self.direct, x_s.at[self.n - RINGS])

    parts = [
        Heads(
            c, ctxb.at[c], sibrecv.at[c],
            (arecv.at[c], bsend.at[c], brecv.at[c], CHUNK // 2) if c < RINGS else None,
            xrecv.at[c - RINGS] if c >= RINGS else None,
        )
        for c in range(N_CHUNK)
    ]
    latent_part = Heads(N_CHUNK, ltb, lsib, None, lrecv)

    for p in range(2):
        load_pair(p).wait()
        qT[:, p * PAIR : (p + 1) * PAIR] = dot(lat[p], wq[...]).astype(BF).T
    for h in range(2):
        m = None
        for j in range(0, TOK, CHUNK):
            m = scores(0, h, j, m)
        mrow[h] = jnp.broadcast_to(m, (8, PAIR))
    pl.semaphore_wait(barrier, N_SEQ - 1 + 4)

    def step(p, _):
        forward(p, True, True)
        return 0

    lax.fori_loop(0, N_PAIR - 2, step, 0)
    forward(N_PAIR - 2, True, False)
    forward(N_PAIR - 1, False, False)
    for p in range(N_PAIR):
        merge(p)
    for h in range(2):
        outs.start(h, out_block)

    grad_scores(0, 0)
    grad_scores(1, 0)
    grad_keys_values(0, 0)
    grad_keys_values(1, 0)
    context_term(0)
    grad_scores(0, 1)
    grad_scores(1, 1)
    grad_keys_values(0, 1)
    parts[0].a()
    grad_keys_values(1, 1)
    context_term(1)
    grad_scores(0, 2)
    grad_scores(0, 3)
    queries.start(0, query_block)
    parts[1].a()
    grad_scores(1, 2)
    grad_scores(1, 3)
    queries.start(1, query_block)
    parts[0].b()
    grad_keys_values(0, 2)
    grad_keys_values(1, 2)
    context_term(2)
    for h in range(2):
        outs.second(h)
    grad_keys_values(0, 3)
    parts[1].b()
    parts[2].a()
    grad_keys_values(1, 3)
    context_term(3)
    queries.second(0)
    parts[3].a()
    queries.second(1)

    def store_context(c):
        rc = pl.ds(c * CHUNK, CHUNK)
        return pltpu.make_async_copy(gc_ref.at[rc], gc_out.at[rc], out_sem.at[c])

    def finish_context(c):
        gc_ref[c * CHUNK : (c + 1) * CHUNK, :] = parts[c].finish().astype(BF)
        store_context(c).start()

    store_attention = pltpu.make_async_copy(att_ref, att_out, out_sem.at[N_CHUNK])
    store_latents = pltpu.make_async_copy(gl_ref, gl_out, out_sem.at[N_CHUNK + 1])

    for h in range(2):
        att_ref[:, h * E : (h + 1) * E] = outs.finish(h).T.astype(BF)
    store_attention.start()

    dq = jnp.concatenate([queries.finish(h) for h in range(2)], axis=0).astype(BF).T
    for n in range(8):
        ltb[n % 2, n // 2] = dot_nt(dq, wq[n * COLS : (n + 1) * COLS, :]).astype(BF)
    latent_part.sib_start()
    finish_context(0)
    latent_part.a()
    for c in range(1, N_CHUNK):
        finish_context(c)
    gl_ref[...] = latent_part.finish().astype(BF)
    store_latents.start()

    wait_bytes(srecv.at[:, pl.ds(1, N_SEQ - 1)], st_s.at[0])
    for part in [*parts, latent_part, outs, queries]:
        part.drain()
    for c in range(N_CHUNK):
        store_context(c).wait()
    store_attention.wait()
    store_latents.wait()


def body(latents, context, offsets, w_query, w_key, w_value, grad_out):
    hbm = pl.BlockSpec(memory_space=pltpu.HBM)
    v, dma = pltpu.VMEM, pltpu.SemaphoreType.DMA
    return pl.pallas_call(
        kernel,
        out_shape=(
            jax.ShapeDtypeStruct((LAT // N_SEQ, COLS), BF),
            jax.ShapeDtypeStruct((LAT // N_SEQ, COLS), BF),
            jax.ShapeDtypeStruct((TOK, COLS), BF),
        ),
        in_specs=[hbm] * 7,
        out_specs=(pl.BlockSpec(memory_space=pl.ANY),) * 3,
        scratch_shapes=[
            v((LAT // N_SEQ, COLS), BF),
            v((LAT // N_SEQ, COLS), BF),
            v((TOK, COLS), BF),
            v((N_PAIR, 1, PAIR), jnp.int32),
            v((N_PAIR, PAIR, WIDE), BF),
            v((WIDE, COLS), BF),
            v((WIDE, 2 * COLS), BF),
            v((LAT, COLS), BF),
            v((COLS, LAT), BF),
            v((TOK, COLS), BF),
            v((TOK, COLS), BF),
            v((COLS, TOK), BF),
            v((2, E + 16, TOK), BF),
            v((COLS, LAT), BF),
            v((2, TOK, LAT), BF),
            v((2, TOK, PAIR), F32),
            v((2, 8, PAIR), F32),
            v((2, 8, LAT), F32),
            v((2, 8, LAT), F32),
            v((N_PAIR, 8, 128), F32),
            v((N_PAIR, N_SEQ, 8, 128), F32),
            v((N_SEQ, COLS, 128), BF),
            v((COLS, LAT), BF),
            v((COLS, LAT), BF),
            v((COLS, LAT), F32),
            v((TOK, 2 * COLS), BF),
            v((2, 2, 4, 512, 128), BF),
            v((2, 2, 3, 512, 128), BF),
            v((2, 2, 4, 128, 128), BF),
            v((2, 2, 3, 128, 128), BF),
            v((N_CHUNK, 2, 4, CHUNK, COLS), BF),
            v((N_CHUNK, 4, CHUNK, COLS), BF),
            v((RINGS, 2, CHUNK // 2, COLS), BF),
            v((RINGS, 2, CHUNK, COLS), BF),
            v((RINGS, 2, CHUNK, COLS), BF),
            v((N_CHUNK - RINGS, 3, CHUNK, COLS), BF),
            v((2, 4, 128, COLS), BF),
            v((4, 128, COLS), BF),
            v((3, 128, COLS), BF),
            dma((17,)),
            dma((1,)),
            dma((N_PAIR,)),
            *[dma((8,))] * 2,
            *[dma((N_CHUNK + 1,))] * 2,
            *[dma((RINGS, 2))] * 4,
            *[dma((N_CHUNK + 1 - RINGS,))] * 2,
            dma((N_CHUNK + 2,)),
        ],
        compiler_params=pltpu.CompilerParams(
            collective_id=0, has_side_effects=True, vmem_limit_bytes=50 * 1024 * 1024
        ),
        cost_estimate=pl.CostEstimate(flops=13_000_000_000, bytes_accessed=20_000_000, transcendentals=4_200_000),
    )(
        *[
            pltpu.with_memory_space_constraint(a, pltpu.HBM)
            for a in (latents, context, offsets.reshape(N_PAIR, 1, PAIR), w_query, w_key, w_value, grad_out)
        ]
    )


def solution(mesh):
    placed = (
        P(),
        P("seq", None),
        P(),
        P(None, "head"),
        P(None, "head"),
        P(None, "head"),
        P(None, "head"),
    )
    return jax.shard_map(
        body,
        mesh=mesh,
        in_specs=placed,
        out_specs=(P("seq", "head"), P("seq", "head"), P("seq", "head")),
        check_vma=False,
    )
```

```python
import functools
import math

import jax
import jax.numpy as jnp
from jax import lax
from jax.experimental import pallas as pl
from jax.experimental.pallas import tpu as pltpu
from jax.sharding import PartitionSpec as P

E = 128
SCALE = E ** (-0.5)
TO_LOG2 = SCALE * math.log2(math.e)
FLOOR = -1e30
N_SEQ = 16
LAT = 2048
TOK = 1024
COLS = 256
WIDE = 2048
PAIR = 256
N_PAIR = LAT // PAIR
CHUNK = 256
N_CHUNK = TOK // CHUNK
CHUNKS = ((0, 128), (128, 128), (256, 256), (512, 256), (768, 256))
N_PART = len(CHUNKS)
MESH = pl.DeviceIdType.MESH
BF = jnp.bfloat16
F32 = jnp.float32

NT = (((1,), (1,)), ((), ()))


def dot(a, b):
    return jnp.dot(a, b, preferred_element_type=F32)


def dot_nt(a, b):
    return lax.dot_general(a, b, NT, preferred_element_type=F32)


class Ring:
    def __init__(self, n, sems, where, ends, total, a_in, b_out, b_in, half):
        self.n, self.sems, self.half = n, sems, half
        self.me, self.right, self.left, self.far = where
        self.ends = ends
        self.total, self.a_in, self.b_out, self.b_in = total, a_in, b_out, b_in

    def copy(self, src, dst, s, r, way):
        return pltpu.make_async_remote_copy(
            src_ref=src, dst_ref=dst, send_sem=s.at[self.n, way], recv_sem=r.at[self.n, way],
            device_id=self.ends[way], device_id_type=MESH)

    def c_a(self, way):
        part = pl.ds(way * self.half, self.half)
        return self.copy(self.total.at[self.far, part], self.a_in.at[way], self.sems[0], self.sems[1], way)

    def c_b(self, way):
        return self.copy(self.b_out.at[way], self.b_in.at[way], self.sems[2], self.sems[3], way)

    def step_a(self):
        for way in range(2):
            self.c_a(way).start()

    def step_b(self):
        for way in range(2):
            self.c_a(way).wait_recv()
            to = (self.right, self.left)[way]
            mine, other = pl.ds(way * self.half, self.half), pl.ds((1 - way) * self.half, self.half)
            self.b_out[way, mine, :] = (self.total[to, mine, :].astype(F32) + self.a_in[way].astype(F32)).astype(BF)
            self.b_out[way, other, :] = self.total[to, other, :]
            self.c_b(way).start()

    def finish(self):
        for way in range(2):
            self.c_b(way).wait_recv()
        return self.total[self.me].astype(F32) + self.b_in[0].astype(F32) + self.b_in[1].astype(F32)

    def drain(self):
        for way in range(2):
            self.c_a(way).wait_send()
            self.c_b(way).wait_send()


def kernel(
    lat_hbm, ctx_hbm, off_hbm, wq_hbm, wk_hbm, wv_hbm, go_hbm,
    att_out, gl_out, gc_out,
    att_ref, gl_ref, gc_ref,
    off_ref, lat, wq, wkv, go,
    goT, k_s, v_s, kT, v1T, qT, wT, sc, mrow,
    mflat, fflat, sbuf, srecv, obuf,
    gosT, fqT, dqT, dkv, tot1, r1, tot2, r2, dqbuf, dqrecv,
    ctxb, sibrecv, arecv, bsend, brecv,
    ltb, lsib, lrecv,
    in_sem, st_s, st_r, f_s, f_r, dq_s, dq_r, sib_s, sib_r, a_s, a_r, b_s, b_r, x_s, x_r, out_sem,
):
    seq = lax.axis_index("seq")
    head = lax.axis_index("head")
    core, x = lax.rem(head, 2), head // 2
    y, z = lax.rem(seq, 4), seq // 4
    ring_sems = (a_s, a_r, b_s, b_r)
    on_x, on_y, on_z = ([lax.rem(at + i, 4) for i in (0, 1, 3, 2)] for at in (x, y, z))
    x_ends = [(seq, i * 2 + core) for i in on_x[1:]]
    y_ends = [(z * 4 + i, head) for i in on_y[1:]]
    z_ends = [(i * 4 + y, head) for i in on_z[1:]]
    sibling = (seq, x * 2 + 1 - core)

    def peer(k):
        return lax.rem(seq + k, N_SEQ)

    def remote(src, dst, ss, rs, to):
        return pltpu.make_async_remote_copy(
            src_ref=src, dst_ref=dst, send_sem=ss, recv_sem=rs, device_id=to, device_id_type=MESH)

    def load(src, dst, n):
        return pltpu.make_async_copy(src, dst, in_sem.at[n])

    def load_context(c):
        rc = pl.ds(c * CHUNK, CHUNK)
        return load(ctx_hbm.at[rc], wT.at[0, rc], 4 + c)

    def load_pair(p):
        return load(lat_hbm.at[pl.ds(p * PAIR, PAIR)], lat.at[p], 8 + p)

    load_k = load(wk_hbm, wkv.at[:, pl.ds(0, COLS)], 0)
    load_v = load(wv_hbm, wkv.at[:, pl.ds(COLS, COLS)], 1)
    load_q = load(wq_hbm, wq, 2)
    def load_grad(p):
        rows = pl.ds(p * PAIR, PAIR)
        return load(go_hbm.at[rows], go.at[rows], 17 + p)

    load_offsets = load(off_hbm, off_ref, 16)
    load_q.start()
    load_pair(0).start()
    load_pair(1).start()
    load_k.start()
    load_v.start()
    load_context(0).start()
    load_context(1).start()
    for p in range(N_PAIR):
        load_grad(p).start()
    load_context(2).start()
    load_context(3).start()

    barrier = pltpu.get_barrier_semaphore()
    for k in range(1, N_SEQ):
        pl.semaphore_signal(barrier, inc=1, device_id=(peer(k), head), device_id_type=MESH)
    for end in [sibling, *x_ends]:
        pl.semaphore_signal(barrier, inc=1, device_id=end, device_id_type=MESH)

    v1T[:, E:, :] = jnp.ones((2, 16, TOK), BF)
    def lanes(p):
        return pl.ds(pl.multiple_of(p * PAIR, PAIR), PAIR)

    def turn(c):
        rc = pl.ds(c * CHUNK, CHUNK)
        kT[:, rc] = k_s[rc, :].T
        vt = v_s[rc, :].T
        for h in range(2):
            v1T[h, 0:E, rc] = vt[h * E : (h + 1) * E, :]

    load_q.wait()
    for p in range(2):
        load_pair(p).wait()
        qT[:, p * PAIR : (p + 1) * PAIR] = dot(lat[p], wq[...]).astype(BF).T
    load_k.wait()
    load_v.wait()
    for c in range(N_CHUNK):
        rc = pl.ds(c * CHUNK, CHUNK)
        load_context(c).wait()
        if c == 0:
            load_offsets.start()
        else:
            load_pair(2 * c).start()
            load_pair(2 * c + 1).start()
        pieces = range(3 * (c - 1), min(3 * c, N_PAIR)) if c else ()
        for p in pieces:
            load_grad(p).wait()
        both = dot(wT[0, rc, :], wkv[...]).astype(BF)
        if c:
            turn(c - 1)
        for p in pieces:
            goT[:, p * PAIR : (p + 1) * PAIR] = go[p * PAIR : (p + 1) * PAIR, :].T
        k_s[rc, :] = both[:, :COLS]
        v_s[rc, :] = both[:, COLS:]
    load_offsets.wait()

    def query(p, acc, n):
        kc = slice(n * 512, (n + 1) * 512)
        return acc + dot(lat[p, :, kc], wq[kc, :])

    def scores(p, h, j, top):
        at = lanes(p)
        hs = slice(h * E, (h + 1) * E)
        s = dot(k_s[j : j + CHUNK, hs], qT[hs, at])
        bound = off_ref[p] - (seq * TOK + j)
        s = jnp.where(lax.broadcasted_iota(jnp.int32, (CHUNK, PAIR), 0) <= bound, s, FLOOR)
        sc[h, j : j + CHUNK, :] = s
        m = jnp.max(s, axis=0, keepdims=True)
        return m if top is None else jnp.maximum(top, m)

    def stat_copy(p, k):
        return remote(sbuf.at[p], srecv.at[p, k], st_s.at[0], st_r.at[p], (peer(k), head))

    def wait_bytes(ref, sem):
        pltpu.make_async_copy(ref, ref, sem).wait()

    def forward(p, ahead, further):
        at = lanes(p)
        top = [mrow[h, 0:1, :] * TO_LOG2 for h in range(2)]
        out, then, acc = [0.0, 0.0], [None, None], 0.0
        if further:
            load_pair(p + 2).wait()
        for n in range(N_CHUNK):
            j = n * CHUNK
            for h in range(2):
                w = jnp.exp2(sc[h, j : j + CHUNK, :] * TO_LOG2 - top[h]).astype(BF)
                wT[h, j : j + CHUNK, at] = w
                out[h] = out[h] + dot(v1T[h, :, j : j + CHUNK], w)
                if ahead:
                    then[h] = scores(p + 1, h, j, then[h])
            if further:
                acc = query(p + 2, acc, n)
        if further:
            qT[:, lanes(p + 2)] = acc.astype(BF).T
        lse, delta = [], []
        for h in range(2):
            hs = slice(h * E, (h + 1) * E)
            total = out[h][E : E + 1]
            o = out[h][:E] / total
            d = jnp.sum(goT[hs, at].astype(F32) * o, axis=0, keepdims=True)
            mflat[h, :, at] = jnp.broadcast_to(top[h], (8, PAIR))
            if ahead:
                mrow[h] = jnp.broadcast_to(then[h], (8, PAIR))
            both = top[h] + jnp.log2(total)
            lse += [both[:, :128], both[:, 128:]]
            delta += [d[:, :128], d[:, 128:]]
            ob = o.astype(BF)
            for half in range(2):
                obuf[2 * p + half, hs, :] = ob[:, half * 128 : (half + 1) * 128]
        sbuf[p] = jnp.concatenate(lse + delta, axis=0)
        for k in range(1, N_SEQ):
            stat_copy(p, k).start()

    def merge(p):
        wait_bytes(srecv.at[p, pl.ds(1, N_SEQ - 1)], st_r.at[p])
        everyone = [sbuf[p]] + [srecv[p, k] for k in range(1, N_SEQ)]
        top = functools.reduce(jnp.maximum, [e[0:4] for e in everyone])
        factors = [jnp.exp2(e[0:4] - top) for e in everyone]
        total = sum(factors)
        delta = sum(e[4:8] * f for e, f in zip(everyone, factors)) / total
        lse = top + jnp.log2(total)
        share = factors[0] / total
        at = slice(p * PAIR, (p + 1) * PAIR)
        for h in range(2):
            hs = slice(h * E, (h + 1) * E)
            rows = [jnp.concatenate([a[2 * h : 2 * h + 1], a[2 * h + 1 : 2 * h + 2]], axis=1) for a in (lse, delta, share)]
            f = jnp.exp2(mflat[h, 0:1, at] - rows[0])
            fflat[h, 0:1, at] = f
            fflat[h, 1:2, at] = rows[1]
            fflat[h, 2:3, at] = rows[2]
            gosT[hs, at] = (goT[hs, at].astype(F32) * f).astype(BF)
            fqT[hs, at] = (qT[hs, at].astype(F32) * f).astype(BF)

    def rows_of(c):
        return pl.ds(*CHUNKS[c])

    def kept(h, c):
        start, size = CHUNKS[c]
        return lat.at[h * N_CHUNK + start // CHUNK, pl.ds(start % CHUNK, size)]

    def grad_scores(h, c):
        hs = slice(h * E, (h + 1) * E)
        rc = rows_of(c)
        if c == 0:
            dp = jnp.concatenate([sc[h, p * 128 : (p + 1) * 128, :] for p in range(N_PAIR)], axis=1)
        else:
            dp = dot(v_s[rc, hs], goT[hs, :])
        ds = (wT[h, rc, :].astype(F32) * (dp - fflat[h, 1:2, :])).astype(BF)
        kept(h, c)[...] = ds
        dq = dot(kT[hs, rc], ds)
        dqT[hs, :] = dq if c == 0 else dqT[hs, :] + dq

    class Blocks:
        axes = ((on_y, y_ends), (on_z, z_ends))

        def copies(self, h, stage):
            on, ends = self.axes[h ^ stage]
            src, dst = ((tot1, r1), (tot2, r2))[stage]
            n = 2 * h + stage
            return [remote(src.at[h, on[d + 1]], dst.at[h, d], f_s.at[n], f_r.at[n], ends[d]) for d in range(3)]

        def start(self, h, block):
            for b in range(N_SEQ):
                to, row = (b % 4, b // 4) if h == 0 else (b // 4, b % 4)
                tot1[h, to, row * 128 : (row + 1) * 128, :] = block(h, b).astype(BF)
            for copy in self.copies(h, 0):
                copy.start()

        def total(self, h, stage):
            src, dst = ((tot1, r1), (tot2, r2))[stage]
            wait_bytes(dst.at[h], f_r.at[2 * h + stage])
            me = self.axes[h ^ stage][0][0]
            return src[h, me].astype(F32) + sum(dst[h, d].astype(F32) for d in range(3))

        def second(self, h):
            got = self.total(h, 0).astype(BF)
            for j in range(4):
                tot2[h, j] = got[j * 128 : (j + 1) * 128, :]
            for copy in self.copies(h, 1):
                copy.start()

        def finish(self, h):
            return self.total(h, 1)

        def drain(self):
            for h in range(2):
                wait_bytes(r1.at[h], f_s.at[2 * h])
                wait_bytes(r2.at[h], f_s.at[2 * h + 1])

    outs = Blocks()

    def out_block(h, b):
        at = slice(b * 128, (b + 1) * 128)
        return obuf[b, h * E : (h + 1) * E, :].astype(F32) * fflat[h, 2:3, at]

    def send_query(h):
        for b in range(N_SEQ):
            at = slice(b * 128, (b + 1) * 128)
            dqbuf[h, b] = (dqT[h * E : (h + 1) * E, at] * (fflat[h, 0:1, at] * SCALE)).astype(BF)
        for k in range(1, N_SEQ):
            remote(dqbuf.at[h, peer(k)], dqrecv.at[h, k], dq_s.at[h], dq_r.at[h], (peer(k), head)).start()

    def own_query(h):
        wait_bytes(dqrecv.at[h, pl.ds(1, N_SEQ - 1)], dq_r.at[h])
        return dqbuf[h, seq].astype(F32) + sum(dqrecv[h, k].astype(F32) for k in range(1, N_SEQ))

    def grad_keys_values(h, c):
        rc = rows_of(c)
        hs = slice(h * E, (h + 1) * E)
        dkv[rc, hs] = (dot_nt(kept(h, c)[...], fqT[hs, :]) * SCALE).astype(BF)
        dkv[rc, COLS + h * E : COLS + (h + 1) * E] = dot_nt(wT[h, rc, :], gosT[hs, :]).astype(BF)

    def term_of(c):
        start, size = CHUNKS[c]
        return ctxb.at[start // CHUNK, :, :, pl.ds(start % CHUNK, size)]

    def context_term(c):
        rc = rows_of(c)
        for n in range(8):
            term_of(c)[n % 2, n // 2] = dot_nt(dkv[rc, :], wkv[n * COLS : (n + 1) * COLS, :]).astype(BF)
        parts[c].sib_start()

    class Heads:
        def __init__(self, n, term, sib, ring):
            self.n, self.sib, self.total = n, sib, term.at[core]
            self.c_sib = remote(term.at[1 - core], sib, sib_s.at[n], sib_r.at[n], sibling)
            self.ring = Ring(n, ring_sems, on_x, x_ends, self.total, *ring) if ring else None

        def copies(self):
            return [remote(self.total.at[on_x[d + 1]], lrecv.at[d], x_s.at[0], x_r.at[0], x_ends[d]) for d in range(3)]

        def sib_start(self):
            self.c_sib.start()

        def a(self):
            self.c_sib.wait_recv()
            for j in range(4):
                self.total[j] = (self.total[j].astype(F32) + self.sib[j].astype(F32)).astype(BF)
            if self.ring:
                self.ring.step_a()
            else:
                for copy in self.copies():
                    copy.start()

        def b(self):
            self.ring.step_b()

        def finish(self):
            if self.ring:
                return self.ring.finish()
            wait_bytes(lrecv, x_r.at[0])
            return self.total[x].astype(F32) + sum(lrecv[d].astype(F32) for d in range(3))

        def drain(self):
            self.c_sib.wait_send()
            if self.ring:
                self.ring.drain()
            else:
                wait_bytes(lrecv, x_s.at[0])

    def part(c):
        start, size = CHUNKS[c]
        block, rc = start // CHUNK, pl.ds(start % CHUNK, size)
        ring = (arecv.at[block, :, pl.ds(start % CHUNK // 2, size // 2)], bsend.at[block, :, rc], brecv.at[block, :, rc])
        return Heads(c, term_of(c), sibrecv.at[block, :, rc], (*ring, size // 2))

    parts = [part(c) for c in range(N_PART)]
    latent_part = Heads(N_PART, ltb, lsib, None)

    turn(N_CHUNK - 1)
    for h in range(2):
        m = None
        for j in range(0, TOK, CHUNK):
            m = scores(0, h, j, m)
        mrow[h] = jnp.broadcast_to(m, (8, PAIR))
    pl.semaphore_wait(barrier, N_SEQ - 1 + 4)

    def step(p, _):
        forward(p, True, True)
        return 0

    lax.fori_loop(0, N_PAIR - 2, step, 0)
    forward(N_PAIR - 2, True, False)
    forward(N_PAIR - 1, False, False)
    for p in range(N_PAIR - 1):
        merge(p)
    for h in range(2):
        hs = slice(h * E, (h + 1) * E)
        for p in range(N_PAIR):
            sc[h, p * 128 : (p + 1) * 128, :] = dot(v_s[0:128, hs], goT[hs, p * PAIR : (p + 1) * PAIR])
    merge(N_PAIR - 1)
    for h in range(2):
        outs.start(h, out_block)

    def both_heads(f, c):
        for h in range(2):
            f(h, c)

    both_heads(grad_scores, 0)
    both_heads(grad_keys_values, 0)
    context_term(0)
    both_heads(grad_scores, 1)
    both_heads(grad_keys_values, 1)
    parts[0].a()
    context_term(1)
    for c in (2, 3, 4):
        grad_scores(0, c)
    send_query(0)
    parts[1].a()
    grad_scores(1, 2)
    grad_keys_values(0, 2)
    parts[0].b()
    grad_keys_values(1, 2)
    context_term(2)
    grad_scores(1, 3)
    grad_scores(1, 4)
    send_query(1)
    parts[2].a()
    parts[1].b()
    both_heads(grad_keys_values, 3)
    context_term(3)
    grad_keys_values(0, 4)
    parts[2].b()
    grad_keys_values(1, 4)
    parts[3].a()
    context_term(4)
    for h in range(2):
        outs.second(h)
    parts[4].a()
    parts[3].b()

    def store_context(c):
        rc = rows_of(c)
        return pltpu.make_async_copy(gc_ref.at[rc], gc_out.at[rc], out_sem.at[c])

    def finish_context(c):
        gc_ref[rows_of(c), :] = parts[c].finish().astype(BF)
        store_context(c).start()

    store_attention = pltpu.make_async_copy(att_ref, att_out, out_sem.at[N_PART])
    store_latents = pltpu.make_async_copy(gl_ref, gl_out, out_sem.at[N_PART + 1])

    dq = jnp.concatenate([own_query(h) for h in range(2)], axis=0).astype(BF).T
    for n in range(8):
        ltb[n % 2, n // 2] = dot_nt(dq, wq[n * COLS : (n + 1) * COLS, :]).astype(BF)
    latent_part.sib_start()
    parts[4].b()

    for h in range(2):
        att_ref[:, h * E : (h + 1) * E] = outs.finish(h).T.astype(BF)
    store_attention.start()
    latent_part.a()
    finish_context(0)
    finish_context(1)
    finish_context(2)
    finish_context(3)
    finish_context(4)
    gl_ref[...] = latent_part.finish().astype(BF)
    store_latents.start()

    wait_bytes(srecv.at[:, pl.ds(1, N_SEQ - 1)], st_s.at[0])
    for h in range(2):
        wait_bytes(dqrecv.at[h, pl.ds(1, N_SEQ - 1)], dq_s.at[h])
    for part in [*parts, latent_part, outs]:
        part.drain()
    for c in range(N_PART):
        store_context(c).wait()
    store_attention.wait()
    store_latents.wait()


def body(latents, context, offsets, w_query, w_key, w_value, grad_out):
    hbm = pl.BlockSpec(memory_space=pltpu.HBM)
    v, dma = pltpu.VMEM, pltpu.SemaphoreType.DMA
    return pl.pallas_call(
        kernel,
        out_shape=(
            jax.ShapeDtypeStruct((LAT // N_SEQ, COLS), BF),
            jax.ShapeDtypeStruct((LAT // N_SEQ, COLS), BF),
            jax.ShapeDtypeStruct((TOK, COLS), BF),
        ),
        in_specs=[hbm] * 7,
        out_specs=(pl.BlockSpec(memory_space=pl.ANY),) * 3,
        scratch_shapes=[
            v((LAT // N_SEQ, COLS), BF),
            v((LAT // N_SEQ, COLS), BF),
            v((TOK, COLS), BF),
            v((N_PAIR, 1, PAIR), jnp.int32),
            v((N_PAIR, PAIR, WIDE), BF),
            v((WIDE, COLS), BF),
            v((WIDE, 2 * COLS), BF),
            v((LAT, COLS), BF),
            v((COLS, LAT), BF),
            v((TOK, COLS), BF),
            v((TOK, COLS), BF),
            v((COLS, TOK), BF),
            v((2, E + 16, TOK), BF),
            v((COLS, LAT), BF),
            v((2, TOK, LAT), BF),
            v((2, TOK, PAIR), F32),
            v((2, 8, PAIR), F32),
            v((2, 8, LAT), F32),
            v((2, 8, LAT), F32),
            v((N_PAIR, 8, 128), F32),
            v((N_PAIR, N_SEQ, 8, 128), F32),
            v((N_SEQ, COLS, 128), BF),
            v((COLS, LAT), BF),
            v((COLS, LAT), BF),
            v((COLS, LAT), F32),
            v((TOK, 2 * COLS), BF),
            v((2, 4, 512, 128), BF),
            v((2, 3, 512, 128), BF),
            v((2, 4, 128, 128), BF),
            v((2, 3, 128, 128), BF),
            v((2, N_SEQ, 128, 128), BF),
            v((2, N_SEQ, 128, 128), BF),
            v((N_CHUNK, 2, 4, CHUNK, COLS), BF),
            v((N_CHUNK, 4, CHUNK, COLS), BF),
            v((N_CHUNK, 2, CHUNK // 2, COLS), BF),
            v((N_CHUNK, 2, CHUNK, COLS), BF),
            v((N_CHUNK, 2, CHUNK, COLS), BF),
            v((2, 4, 128, COLS), BF),
            v((4, 128, COLS), BF),
            v((3, 128, COLS), BF),
            dma((25,)),
            dma((1,)),
            dma((N_PAIR,)),
            *[dma((4,))] * 2,
            *[dma((2,))] * 2,
            *[dma((N_PART + 1,))] * 2,
            *[dma((N_PART, 2))] * 4,
            *[dma((1,))] * 2,
            dma((N_PART + 2,)),
        ],
        compiler_params=pltpu.CompilerParams(
            collective_id=0, has_side_effects=True, vmem_limit_bytes=50 * 1024 * 1024
        ),
        cost_estimate=pl.CostEstimate(flops=13_000_000_000, bytes_accessed=20_000_000, transcendentals=4_200_000),
    )(
        *[
            pltpu.with_memory_space_constraint(a, pltpu.HBM)
            for a in (latents, context, offsets.reshape(N_PAIR, 1, PAIR), w_query, w_key, w_value, grad_out)
        ]
    )


def solution(mesh):
    placed = (
        P(),
        P("seq", None),
        P(),
        P(None, "head"),
        P(None, "head"),
        P(None, "head"),
        P(None, "head"),
    )
    return jax.shard_map(
        body,
        mesh=mesh,
        in_specs=placed,
        out_specs=(P("seq", "head"), P("seq", "head"), P("seq", "head")),
        check_vma=False,
    )
```

```python
import functools
import math

import jax
import jax.numpy as jnp
from jax import lax
from jax.experimental import pallas as pl
from jax.experimental.pallas import tpu as pltpu
from jax.sharding import PartitionSpec as P

E = 128
SCALE = E ** (-0.5)
TO_LOG2 = SCALE * math.log2(math.e)
FLOOR = -1e30
N_SEQ = 16
LAT = 2048
TOK = 1024
COLS = 256
WIDE = 2048
PAIR = 256
N_PAIR = LAT // PAIR
CHUNK = 256
N_CHUNK = TOK // CHUNK
CHUNKS = ((0, 128), (128, 128), (256, 256), (512, 256), (768, 256))
N_PART = len(CHUNKS)
MESH = pl.DeviceIdType.MESH
BF = jnp.bfloat16
F32 = jnp.float32

NT = (((1,), (1,)), ((), ()))


def dot(a, b):
    return jnp.dot(a, b, preferred_element_type=F32)


def dot_nt(a, b):
    return lax.dot_general(a, b, NT, preferred_element_type=F32)


class Ring:
    def __init__(self, n, sems, where, ends, total, a_in, b_out, b_in, half):
        self.n, self.sems, self.half = n, sems, half
        self.me, self.right, self.left, self.far = where
        self.ends = ends
        self.total, self.a_in, self.b_out, self.b_in = total, a_in, b_out, b_in

    def copy(self, src, dst, s, r, way):
        return pltpu.make_async_remote_copy(
            src_ref=src, dst_ref=dst, send_sem=s.at[self.n // N_PART], recv_sem=r.at[self.n, way],
            device_id=self.ends[way], device_id_type=MESH)

    def c_a(self, way):
        part = pl.ds(way * self.half, self.half)
        return self.copy(self.total.at[self.far, part], self.a_in.at[way], self.sems[0], self.sems[1], way)

    def c_b(self, way):
        return self.copy(self.b_out.at[way], self.b_in.at[way], self.sems[2], self.sems[3], way)

    def step_a(self):
        for way in range(2):
            self.c_a(way).start()

    def step_b(self):
        for way in range(2):
            self.c_a(way).wait_recv()
            to = (self.right, self.left)[way]
            mine, other = pl.ds(way * self.half, self.half), pl.ds((1 - way) * self.half, self.half)
            self.b_out[way, mine, :] = (self.total[to, mine, :].astype(F32) + self.a_in[way].astype(F32)).astype(BF)
            self.b_out[way, other, :] = self.total[to, other, :]
            self.c_b(way).start()

    def finish(self):
        for way in range(2):
            self.c_b(way).wait_recv()
        return self.total[self.me].astype(F32) + self.b_in[0].astype(F32) + self.b_in[1].astype(F32)


def kernel(
    lat_hbm, ctx_hbm, off_hbm, wq_hbm, wk_hbm, wv_hbm, go_hbm,
    att_out, gl_out, gc_out,
    att_ref, gl_ref, gc_ref,
    off_ref, lat, wq, wkv, go,
    goT, k_s, v_s, kT, v1T, qT, wT, sc, sc1, mrow,
    mflat, fflat, sbuf, srecv, obuf,
    gosT, fqT, dqT, dkv, tot1, r1, tot2, r2, dqbuf, dqrecv,
    ctxb, sibrecv, arecv, bsend, brecv,
    ltb, lsib, larecv, lbsend, lbrecv,
    in_sem, st_s, st_r, f_s, f_r, dq_s, dq_r, sib_s, sib_r, a_s, a_r, b_s, b_r, out_sem,
):
    seq = lax.axis_index("seq")
    head = lax.axis_index("head")
    core, x = lax.rem(head, 2), head // 2
    y, z = lax.rem(seq, 4), seq // 4
    ring_sems = (a_s, a_r, b_s, b_r)
    on_x, on_y, on_z = ([lax.rem(at + i, 4) for i in (0, 1, 3, 2)] for at in (x, y, z))
    x_ends = [(seq, i * 2 + core) for i in on_x[1:]]
    y_ends = [(z * 4 + i, head) for i in on_y[1:]]
    z_ends = [(i * 4 + y, head) for i in on_z[1:]]
    sibling = (seq, x * 2 + 1 - core)

    def peer(k):
        return lax.rem(seq + k, N_SEQ)

    def remote(src, dst, ss, rs, to):
        return pltpu.make_async_remote_copy(
            src_ref=src, dst_ref=dst, send_sem=ss, recv_sem=rs, device_id=to, device_id_type=MESH)

    def load(src, dst, n):
        return pltpu.make_async_copy(src, dst, in_sem.at[n])

    def load_context(c):
        rc = pl.ds(c * CHUNK, CHUNK)
        return load(ctx_hbm.at[rc], wT.at[0, rc], 4 + c)

    def load_pair(p):
        return load(lat_hbm.at[pl.ds(p * PAIR, PAIR)], lat.at[p], 8 + p)

    load_k = load(wk_hbm, wkv.at[:, pl.ds(0, COLS)], 0)
    load_v = load(wv_hbm, wkv.at[:, pl.ds(COLS, COLS)], 1)
    load_q = load(wq_hbm, wq, 2)
    def load_grad(g):
        rows = pl.ds(g * 3 * PAIR, min(3, N_PAIR - 3 * g) * PAIR)
        return load(go_hbm.at[rows], go.at[rows], 17 + g)

    load_offsets = load(off_hbm, off_ref, 16)
    load_q.start()
    load_pair(0).start()
    load_pair(1).start()
    load_k.start()
    load_v.start()
    load_context(0).start()
    load_context(1).start()
    for g in range(3):
        load_grad(g).start()
    load_context(2).start()
    load_context(3).start()

    barrier = pltpu.get_barrier_semaphore()
    for k in range(1, N_SEQ):
        pl.semaphore_signal(barrier, inc=1, device_id=(peer(k), head), device_id_type=MESH)
    for end in [sibling, *x_ends]:
        pl.semaphore_signal(barrier, inc=1, device_id=end, device_id_type=MESH)

    v1T[:, E:, :] = jnp.ones((2, 16, TOK), BF)
    def lanes(p):
        return pl.ds(pl.multiple_of(p * PAIR, PAIR), PAIR)

    def turn(c):
        rc = pl.ds(c * CHUNK, CHUNK)
        kT[:, rc] = k_s[rc, :].T
        vt = v_s[rc, :].T
        for h in range(2):
            v1T[h, 0:E, rc] = vt[h * E : (h + 1) * E, :]

    load_q.wait()
    for p in range(2):
        load_pair(p).wait()
        qT[:, p * PAIR : (p + 1) * PAIR] = dot(lat[p], wq[...]).astype(BF).T
    load_k.wait()
    load_v.wait()
    load_offsets.start()
    for c in range(2, N_PAIR):
        load_pair(c).start()

    def turn_grad(pieces):
        for p in pieces:
            goT[:, p * PAIR : (p + 1) * PAIR] = go[p * PAIR : (p + 1) * PAIR, :].T

    for n in range(2):
        rc = pl.ds(2 * n * CHUNK, 2 * CHUNK)
        load_context(2 * n).wait()
        load_context(2 * n + 1).wait()
        for g in range(3) if n else ():
            load_grad(g).wait()
        both = dot(wT[0, rc, :], wkv[...]).astype(BF)
        if n:
            turn(0)
            turn(1)
            turn_grad(range(N_PAIR))
        k_s[rc, :] = both[:, :COLS]
        v_s[rc, :] = both[:, COLS:]
    turn(2)
    load_offsets.wait()

    def query(p, acc, n):
        kc = slice(n * 512, (n + 1) * 512)
        return acc + dot(lat[p, :, kc], wq[kc, :])

    def scores(p, h, j, top):
        at = lanes(p)
        hs = slice(h * E, (h + 1) * E)
        s = dot(k_s[j : j + CHUNK, hs], qT[hs, at])
        bound = off_ref[p] - (seq * TOK + j)
        s = jnp.where(lax.broadcasted_iota(jnp.int32, (CHUNK, PAIR), 0) <= bound, s, FLOOR)
        sc[h, j : j + CHUNK, :] = s
        m = jnp.max(s, axis=0, keepdims=True)
        return m if top is None else jnp.maximum(top, m)

    def stat_copy(p, k):
        return remote(sbuf.at[p], srecv.at[p, k], st_s.at[0], st_r.at[p], (peer(k), head))

    def wait_bytes(ref, sem):
        pltpu.make_async_copy(ref, ref, sem).wait()

    def forward(p, ahead, further):
        at = lanes(p)
        top = [mrow[h, 0:1, :] * TO_LOG2 for h in range(2)]
        out, then, acc = [0.0, 0.0], [None, None], 0.0
        if further:
            load_pair(p + 2).wait()
        for n in range(N_CHUNK):
            j = n * CHUNK
            for h in range(2):
                w = jnp.exp2(sc[h, j : j + CHUNK, :] * TO_LOG2 - top[h]).astype(BF)
                wT[h, j : j + CHUNK, at] = w
                out[h] = out[h] + dot(v1T[h, :, j : j + CHUNK], w)
                if ahead:
                    then[h] = scores(p + 1, h, j, then[h])
            if further:
                acc = query(p + 2, acc, n)
        if further:
            qT[:, lanes(p + 2)] = acc.astype(BF).T
        lse, delta = [], []
        for h in range(2):
            hs = slice(h * E, (h + 1) * E)
            total = out[h][E : E + 1]
            o = out[h][:E] / total
            d = jnp.sum(goT[hs, at].astype(F32) * o, axis=0, keepdims=True)
            mflat[h, :, at] = jnp.broadcast_to(top[h], (8, PAIR))
            if ahead:
                mrow[h] = jnp.broadcast_to(then[h], (8, PAIR))
            both = top[h] + jnp.log2(total)
            lse += [both[:, :128], both[:, 128:]]
            delta += [d[:, :128], d[:, 128:]]
            ob = o.astype(BF)
            for half in range(2):
                obuf[2 * p + half, hs, :] = ob[:, half * 128 : (half + 1) * 128]
        sbuf[p] = jnp.concatenate(lse + delta, axis=0)
        for k in range(1, N_SEQ):
            stat_copy(p, k).start()

    def merge(p):
        wait_bytes(srecv.at[p, pl.ds(1, N_SEQ - 1)], st_r.at[p])
        everyone = [sbuf[p]] + [srecv[p, k] for k in range(1, N_SEQ)]
        top = functools.reduce(jnp.maximum, [e[0:4] for e in everyone])
        factors = [jnp.exp2(e[0:4] - top) for e in everyone]
        total = sum(factors)
        delta = sum(e[4:8] * f for e, f in zip(everyone, factors)) / total
        lse = top + jnp.log2(total)
        share = factors[0] / total
        at = slice(p * PAIR, (p + 1) * PAIR)
        for h in range(2):
            hs = slice(h * E, (h + 1) * E)
            rows = [jnp.concatenate([a[2 * h : 2 * h + 1], a[2 * h + 1 : 2 * h + 2]], axis=1) for a in (lse, delta, share)]
            f = jnp.exp2(mflat[h, 0:1, at] - rows[0])
            fflat[h, 0:1, at] = f
            fflat[h, 1:2, at] = rows[1]
            fflat[h, 2:3, at] = rows[2]
            gosT[hs, at] = (goT[hs, at].astype(F32) * f).astype(BF)
            fqT[hs, at] = (qT[hs, at].astype(F32) * f).astype(BF)

    def rows_of(c):
        return pl.ds(*CHUNKS[c])

    def kept(h, c):
        start, size = CHUNKS[c]
        return lat.at[h * N_CHUNK + start // CHUNK, pl.ds(start % CHUNK, size)]

    def grad_scores(h, c):
        hs = slice(h * E, (h + 1) * E)
        rc = rows_of(c)
        if c < 2:
            dp = jnp.concatenate([early[c][h, p * 128 : (p + 1) * 128, :] for p in range(N_PAIR)], axis=1)
        else:
            dp = dot(v_s[rc, hs], goT[hs, :])
        ds = (wT[h, rc, :].astype(F32) * (dp - fflat[h, 1:2, :])).astype(BF)
        kept(h, c)[...] = ds
        dq = dot(kT[hs, rc], ds)
        dqT[hs, :] = dq if c == 0 else dqT[hs, :] + dq

    class Blocks:
        axes = ((on_y, y_ends), (on_z, z_ends))

        def copies(self, h, stage):
            on, ends = self.axes[h ^ stage]
            src, dst = ((tot1, r1), (tot2, r2))[stage]
            n = 2 * h + stage
            return [remote(src.at[h, on[d + 1]], dst.at[h, d], f_s.at[n], f_r.at[n], ends[d]) for d in range(3)]

        def start(self, h, block):
            for b in range(N_SEQ):
                to, row = (b % 4, b // 4) if h == 0 else (b // 4, b % 4)
                tot1[h, to, row * 128 : (row + 1) * 128, :] = block(h, b).astype(BF)
            for copy in self.copies(h, 0):
                copy.start()

        def total(self, h, stage):
            src, dst = ((tot1, r1), (tot2, r2))[stage]
            wait_bytes(dst.at[h], f_r.at[2 * h + stage])
            me = self.axes[h ^ stage][0][0]
            return src[h, me].astype(F32) + sum(dst[h, d].astype(F32) for d in range(3))

        def second(self, h):
            got = self.total(h, 0).astype(BF)
            for j in range(4):
                tot2[h, j] = got[j * 128 : (j + 1) * 128, :]
            for copy in self.copies(h, 1):
                copy.start()

        def finish(self, h):
            return self.total(h, 1)

        def drain(self):
            for h in range(2):
                wait_bytes(r1.at[h], f_s.at[2 * h])
                wait_bytes(r2.at[h], f_s.at[2 * h + 1])

    outs = Blocks()

    def out_block(h, b):
        at = slice(b * 128, (b + 1) * 128)
        return obuf[b, h * E : (h + 1) * E, :].astype(F32) * fflat[h, 2:3, at]

    def send_query(h):
        for b in range(N_SEQ):
            at = slice(b * 128, (b + 1) * 128)
            dqbuf[h, b] = (dqT[h * E : (h + 1) * E, at] * (fflat[h, 0:1, at] * SCALE)).astype(BF)
        for k in range(1, N_SEQ):
            remote(dqbuf.at[h, peer(k)], dqrecv.at[h, k], dq_s.at[h], dq_r.at[h], (peer(k), head)).start()

    def own_query(h):
        wait_bytes(dqrecv.at[h, pl.ds(1, N_SEQ - 1)], dq_r.at[h])
        return dqbuf[h, seq].astype(F32) + sum(dqrecv[h, k].astype(F32) for k in range(1, N_SEQ))

    def grad_keys_values(h, c):
        rc = rows_of(c)
        hs = slice(h * E, (h + 1) * E)
        dkv[rc, hs] = (dot_nt(kept(h, c)[...], fqT[hs, :]) * SCALE).astype(BF)
        dkv[rc, COLS + h * E : COLS + (h + 1) * E] = dot_nt(wT[h, rc, :], gosT[hs, :]).astype(BF)

    def term_of(c):
        start, size = CHUNKS[c]
        return ctxb.at[start // CHUNK, :, :, pl.ds(start % CHUNK, size)]

    def context_term(c):
        rc = rows_of(c)
        for n in range(8):
            term_of(c)[n % 2, n // 2] = dot_nt(dkv[rc, :], wkv[n * COLS : (n + 1) * COLS, :]).astype(BF)
        parts[c].sib_start()

    class Heads:
        def __init__(self, n, term, sib, ring):
            self.n, self.sib, self.total = n, sib, term.at[core]
            self.c_sib = remote(term.at[1 - core], sib, sib_s.at[n // N_PART], sib_r.at[n], sibling)
            self.ring = Ring(n, ring_sems, on_x, x_ends, self.total, *ring)

        def sib_start(self):
            self.c_sib.start()

        def a(self):
            self.c_sib.wait_recv()
            for j in range(4):
                self.total[j] = (self.total[j].astype(F32) + self.sib[j].astype(F32)).astype(BF)
            self.ring.step_a()

        def b(self):
            self.ring.step_b()

        def finish(self):
            return self.ring.finish()

    def part(c):
        start, size = CHUNKS[c]
        block, rc = start // CHUNK, pl.ds(start % CHUNK, size)
        ring = (arecv.at[block, :, pl.ds(start % CHUNK // 2, size // 2)], bsend.at[block, :, rc], brecv.at[block, :, rc])
        return Heads(c, term_of(c), sibrecv.at[block, :, rc], (*ring, size // 2))

    parts = [part(c) for c in range(N_PART)]
    latent_part = Heads(N_PART, ltb, lsib, (larecv, lbsend, lbrecv, 64))

    turn(N_CHUNK - 1)
    for h in range(2):
        m = None
        for j in range(0, TOK, CHUNK):
            m = scores(0, h, j, m)
        mrow[h] = jnp.broadcast_to(m, (8, PAIR))
    pl.semaphore_wait(barrier, N_SEQ - 1 + 4)

    def step(p, _):
        forward(p, True, True)
        return 0

    lax.fori_loop(0, N_PAIR - 2, step, 0)
    forward(N_PAIR - 2, True, False)
    forward(N_PAIR - 1, False, False)
    for p in range(N_PAIR - 1):
        merge(p)
    early = (sc, sc1)
    for c in range(2):
        for h in range(2):
            hs = slice(h * E, (h + 1) * E)
            for p in range(N_PAIR):
                early[c][h, p * 128 : (p + 1) * 128, :] = dot(v_s[rows_of(c), hs], goT[hs, p * PAIR : (p + 1) * PAIR])
    merge(N_PAIR - 1)
    for h in range(2):
        outs.start(h, out_block)

    def both_heads(f, c):
        for h in range(2):
            f(h, c)

    both_heads(grad_scores, 0)
    both_heads(grad_keys_values, 0)
    context_term(0)
    both_heads(grad_scores, 1)
    both_heads(grad_keys_values, 1)
    context_term(1)
    parts[0].a()
    for c in (2, 3, 4):
        grad_scores(0, c)
    send_query(0)
    parts[1].a()
    grad_scores(1, 2)
    grad_keys_values(0, 2)
    parts[0].b()
    grad_keys_values(1, 2)
    context_term(2)
    grad_scores(1, 3)
    grad_scores(1, 4)
    send_query(1)
    grad_keys_values(0, 3)
    parts[1].b()
    parts[2].a()
    grad_keys_values(1, 3)
    context_term(3)
    both_heads(grad_keys_values, 4)
    parts[3].a()
    context_term(4)
    parts[2].b()
    for h in range(2):
        outs.second(h)
    parts[4].a()
    parts[3].b()

    def store_context(c):
        rc = rows_of(c)
        return pltpu.make_async_copy(gc_ref.at[rc], gc_out.at[rc], out_sem.at[c])

    def finish_context(c):
        gc_ref[rows_of(c), :] = parts[c].finish().astype(BF)
        store_context(c).start()

    store_attention = pltpu.make_async_copy(att_ref, att_out, out_sem.at[N_PART])
    store_latents = pltpu.make_async_copy(gl_ref, gl_out, out_sem.at[N_PART + 1])

    dq = jnp.concatenate([own_query(h) for h in range(2)], axis=0).astype(BF).T
    for n in range(8):
        ltb[n % 2, n // 2] = dot_nt(dq, wq[n * COLS : (n + 1) * COLS, :]).astype(BF)
    latent_part.sib_start()

    for h in range(2):
        att_ref[:, h * E : (h + 1) * E] = outs.finish(h).T.astype(BF)
    store_attention.start()
    latent_part.a()
    parts[4].b()
    finish_context(0)
    finish_context(1)
    finish_context(2)
    latent_part.b()
    finish_context(3)
    finish_context(4)
    gl_ref[...] = latent_part.finish().astype(BF)
    store_latents.start()

    wait_bytes(srecv.at[:, pl.ds(1, N_SEQ - 1)], st_s.at[0])
    for h in range(2):
        wait_bytes(dqrecv.at[h, pl.ds(1, N_SEQ - 1)], dq_s.at[h])
    for n, sent in enumerate(((sibrecv, arecv, brecv), (lsib, larecv, lbrecv))):
        for ref, sem in zip(sent, (sib_s, a_s, b_s)):
            wait_bytes(ref, sem.at[n])
    outs.drain()
    for c in range(N_PART):
        store_context(c).wait()
    store_attention.wait()
    store_latents.wait()


def body(latents, context, offsets, w_query, w_key, w_value, grad_out):
    hbm = pl.BlockSpec(memory_space=pltpu.HBM)
    v, dma = pltpu.VMEM, pltpu.SemaphoreType.DMA
    return pl.pallas_call(
        kernel,
        out_shape=(
            jax.ShapeDtypeStruct((LAT // N_SEQ, COLS), BF),
            jax.ShapeDtypeStruct((LAT // N_SEQ, COLS), BF),
            jax.ShapeDtypeStruct((TOK, COLS), BF),
        ),
        in_specs=[hbm] * 7,
        out_specs=(pl.BlockSpec(memory_space=pl.ANY),) * 3,
        scratch_shapes=[
            v((LAT // N_SEQ, COLS), BF),
            v((LAT // N_SEQ, COLS), BF),
            v((TOK, COLS), BF),
            v((N_PAIR, 1, PAIR), jnp.int32),
            v((N_PAIR, PAIR, WIDE), BF),
            v((WIDE, COLS), BF),
            v((WIDE, 2 * COLS), BF),
            v((LAT, COLS), BF),
            v((COLS, LAT), BF),
            v((TOK, COLS), BF),
            v((TOK, COLS), BF),
            v((COLS, TOK), BF),
            v((2, E + 16, TOK), BF),
            v((COLS, LAT), BF),
            v((2, TOK, LAT), BF),
            v((2, TOK, PAIR), F32),
            v((2, TOK, PAIR), F32),
            v((2, 8, PAIR), F32),
            v((2, 8, LAT), F32),
            v((2, 8, LAT), F32),
            v((N_PAIR, 8, 128), F32),
            v((N_PAIR, N_SEQ, 8, 128), F32),
            v((N_SEQ, COLS, 128), BF),
            v((COLS, LAT), BF),
            v((COLS, LAT), BF),
            v((COLS, LAT), F32),
            v((TOK, 2 * COLS), BF),
            v((2, 4, 512, 128), BF),
            v((2, 3, 512, 128), BF),
            v((2, 4, 128, 128), BF),
            v((2, 3, 128, 128), BF),
            v((2, N_SEQ, 128, 128), BF),
            v((2, N_SEQ, 128, 128), BF),
            v((N_CHUNK, 2, 4, CHUNK, COLS), BF),
            v((N_CHUNK, 4, CHUNK, COLS), BF),
            v((N_CHUNK, 2, CHUNK // 2, COLS), BF),
            v((N_CHUNK, 2, CHUNK, COLS), BF),
            v((N_CHUNK, 2, CHUNK, COLS), BF),
            v((2, 4, 128, COLS), BF),
            v((4, 128, COLS), BF),
            v((2, 64, COLS), BF),
            v((2, 128, COLS), BF),
            v((2, 128, COLS), BF),
            dma((20,)),
            dma((1,)),
            dma((N_PAIR,)),
            *[dma((4,))] * 2,
            *[dma((2,))] * 2,
            dma((2,)),
            dma((N_PART + 1,)),
            *[dma((2,)), dma((N_PART + 1, 2))] * 2,
            dma((N_PART + 2,)),
        ],
        compiler_params=pltpu.CompilerParams(
            collective_id=0, has_side_effects=True, vmem_limit_bytes=52 * 1024 * 1024
        ),
        cost_estimate=pl.CostEstimate(flops=13_000_000_000, bytes_accessed=20_000_000, transcendentals=4_200_000),
    )(
        *[
            pltpu.with_memory_space_constraint(a, pltpu.HBM)
            for a in (latents, context, offsets.reshape(N_PAIR, 1, PAIR), w_query, w_key, w_value, grad_out)
        ]
    )


def solution(mesh):
    placed = (
        P(),
        P("seq", None),
        P(),
        P(None, "head"),
        P(None, "head"),
        P(None, "head"),
        P(None, "head"),
    )
    return jax.shard_map(
        body,
        mesh=mesh,
        in_specs=placed,
        out_specs=(P("seq", "head"), P("seq", "head"), P("seq", "head")),
        check_vma=False,
    )
```

```python
import functools
import math

import jax
import jax.numpy as jnp
from jax import lax
from jax.experimental import pallas as pl
from jax.experimental.pallas import tpu as pltpu
from jax.sharding import PartitionSpec as P

E = 128
SCALE = E ** (-0.5)
TO_LOG2 = SCALE * math.log2(math.e)
FLOOR = -1e30
N_SEQ = 16
LAT = 2048
TOK = 1024
COLS = 256
WIDE = 2048
PAIR = 256
N_PAIR = LAT // PAIR
CHUNK = 256
N_CHUNK = TOK // CHUNK
CHUNKS = ((0, 128), (128, 128), (256, 256), (512, 256), (768, 256))
N_PART = len(CHUNKS)
MESH = pl.DeviceIdType.MESH
BF = jnp.bfloat16
F32 = jnp.float32

NT = (((1,), (1,)), ((), ()))


def dot(a, b):
    return jnp.dot(a, b, preferred_element_type=F32)


def dot_nt(a, b):
    return lax.dot_general(a, b, NT, preferred_element_type=F32)


class Ring:
    def __init__(self, n, sems, where, ends, total, a_in, b_out, b_in, half):
        self.n, self.sems, self.half = n, sems, half
        self.me, self.right, self.left, self.far = where
        self.ends = ends
        self.total, self.a_in, self.b_out, self.b_in = total, a_in, b_out, b_in

    def copy(self, src, dst, s, r, way):
        return pltpu.make_async_remote_copy(
            src_ref=src, dst_ref=dst, send_sem=s.at[self.n // N_PART], recv_sem=r.at[self.n, way],
            device_id=self.ends[way], device_id_type=MESH)

    def c_a(self, way):
        part = pl.ds(way * self.half, self.half)
        return self.copy(self.total.at[self.far, part], self.a_in.at[way], self.sems[0], self.sems[1], way)

    def c_b(self, way):
        return self.copy(self.b_out.at[way], self.b_in.at[way], self.sems[2], self.sems[3], way)

    def step_a(self):
        for way in range(2):
            self.c_a(way).start()

    def step_b(self):
        for way in range(2):
            self.c_a(way).wait_recv()
            to = (self.right, self.left)[way]
            mine, other = pl.ds(way * self.half, self.half), pl.ds((1 - way) * self.half, self.half)
            self.b_out[way, mine, :] = (self.total[to, mine, :].astype(F32) + self.a_in[way].astype(F32)).astype(BF)
            self.b_out[way, other, :] = self.total[to, other, :]
            self.c_b(way).start()

    def finish(self):
        for way in range(2):
            self.c_b(way).wait_recv()
        return self.total[self.me].astype(F32) + self.b_in[0].astype(F32) + self.b_in[1].astype(F32)


def kernel(
    lat_hbm, ctx_hbm, off_hbm, wq_hbm, wk_hbm, wv_hbm, go_hbm,
    att_out, gl_out, gc_out,
    att_ref, gl_ref, gc_ref,
    off_ref, lat, wq, wkv, go,
    goT, k_s, v_s, kT, v1T, qT, wT, sc, sc1, mrow,
    mflat, fflat, sbuf, srecv, obuf,
    gosT, fqT, dqT, dkv, tot1, r1, tot2, r2, dqbuf, dqrecv,
    ctxb, sibrecv, arecv, bsend, brecv,
    ltb, lsib, larecv, lbsend, lbrecv,
    in_sem, st_s, st_r, f_s, f_r, dq_s, dq_r, sib_s, sib_r, a_s, a_r, b_s, b_r, out_sem,
):
    seq = lax.axis_index("seq")
    head = lax.axis_index("head")
    core, x = lax.rem(head, 2), head // 2
    y, z = lax.rem(seq, 4), seq // 4
    ring_sems = (a_s, a_r, b_s, b_r)
    on_x, on_y, on_z = ([lax.rem(at + i, 4) for i in (0, 1, 3, 2)] for at in (x, y, z))
    x_ends = [(seq, i * 2 + core) for i in on_x[1:]]
    y_ends = [(z * 4 + i, head) for i in on_y[1:]]
    z_ends = [(i * 4 + y, head) for i in on_z[1:]]
    sibling = (seq, x * 2 + 1 - core)

    def peer(k):
        return lax.rem(seq + k, N_SEQ)

    def remote(src, dst, ss, rs, to):
        return pltpu.make_async_remote_copy(
            src_ref=src, dst_ref=dst, send_sem=ss, recv_sem=rs, device_id=to, device_id_type=MESH)

    def load(src, dst, n):
        return pltpu.make_async_copy(src, dst, in_sem.at[n])

    def load_context(c):
        rc = pl.ds(c * CHUNK, CHUNK)
        return load(ctx_hbm.at[rc], wT.at[0, rc], 4 + c)

    def load_pair(p):
        return load(lat_hbm.at[pl.ds(p * PAIR, PAIR)], lat.at[p], 8 + p)

    load_k = load(wk_hbm, wkv.at[:, pl.ds(0, COLS)], 0)
    load_v = load(wv_hbm, wkv.at[:, pl.ds(COLS, COLS)], 1)
    load_q = load(wq_hbm, wq, 2)
    def load_grad(g):
        rows = pl.ds(g * 3 * PAIR, min(3, N_PAIR - 3 * g) * PAIR)
        return load(go_hbm.at[rows], go.at[rows], 17 + g)

    load_offsets = load(off_hbm, off_ref, 16)
    load_q.start()
    load_pair(0).start()
    load_pair(1).start()
    load_k.start()
    load_v.start()
    load_context(0).start()
    load_context(1).start()
    for g in range(3):
        load_grad(g).start()
    load_context(2).start()
    load_context(3).start()

    barrier = pltpu.get_barrier_semaphore()
    for k in range(1, N_SEQ):
        pl.semaphore_signal(barrier, inc=1, device_id=(peer(k), head), device_id_type=MESH)
    for end in [sibling, *x_ends]:
        pl.semaphore_signal(barrier, inc=1, device_id=end, device_id_type=MESH)

    v1T[:, E:, :] = jnp.ones((2, 16, TOK), BF)
    def lanes(p):
        return pl.ds(pl.multiple_of(p * PAIR, PAIR), PAIR)

    def turn(c):
        rc = pl.ds(c * CHUNK, CHUNK)
        kT[:, rc] = k_s[rc, :].T
        vt = v_s[rc, :].T
        for h in range(2):
            v1T[h, 0:E, rc] = vt[h * E : (h + 1) * E, :]

    load_q.wait()
    load_pair(0).wait()
    load_pair(1).wait()
    qT[:, 0 : 2 * PAIR] = dot(lat[0:2].reshape(2 * PAIR, WIDE), wq[...]).astype(BF).T
    load_k.wait()
    load_v.wait()
    load_offsets.start()
    for c in range(2, N_PAIR):
        load_pair(c).start()

    def turn_grad(pieces):
        for p in pieces:
            goT[:, p * PAIR : (p + 1) * PAIR] = go[p * PAIR : (p + 1) * PAIR, :].T

    for n in range(2):
        rc = pl.ds(2 * n * CHUNK, 2 * CHUNK)
        load_context(2 * n).wait()
        load_context(2 * n + 1).wait()
        for g in range(3) if n else ():
            load_grad(g).wait()
        both = dot(wT[0, rc, :], wkv[...]).astype(BF)
        if n:
            turn(0)
            turn(1)
            turn_grad(range(N_PAIR))
        k_s[rc, :] = both[:, :COLS]
        v_s[rc, :] = both[:, COLS:]
    turn(2)
    load_offsets.wait()

    def query(p, acc, n):
        kc = slice(n * 512, (n + 1) * 512)
        return acc + dot(lat[p, :, kc], wq[kc, :])

    def scores(p, h, j, top):
        at = lanes(p)
        hs = slice(h * E, (h + 1) * E)
        s = dot(k_s[j : j + CHUNK, hs], qT[hs, at])
        bound = off_ref[p] - (seq * TOK + j)
        s = jnp.where(lax.broadcasted_iota(jnp.int32, (CHUNK, PAIR), 0) <= bound, s, FLOOR)
        sc[h, j : j + CHUNK, :] = s
        m = jnp.max(s, axis=0, keepdims=True)
        return m if top is None else jnp.maximum(top, m)

    def stat_copy(p, k):
        return remote(sbuf.at[p], srecv.at[p, k], st_s.at[0], st_r.at[p], (peer(k), head))

    def wait_bytes(ref, sem):
        pltpu.make_async_copy(ref, ref, sem).wait()

    def forward(p, ahead, further):
        at = lanes(p)
        top = [mrow[h, 0:1, :] * TO_LOG2 for h in range(2)]
        out, then, acc = [0.0, 0.0], [None, None], 0.0
        if further:
            load_pair(p + 2).wait()
        for n in range(N_CHUNK):
            j = n * CHUNK
            for h in range(2):
                w = jnp.exp2(sc[h, j : j + CHUNK, :] * TO_LOG2 - top[h]).astype(BF)
                wT[h, j : j + CHUNK, at] = w
                out[h] = out[h] + dot(v1T[h, :, j : j + CHUNK], w)
                if ahead:
                    then[h] = scores(p + 1, h, j, then[h])
            if further:
                acc = query(p + 2, acc, n)
        if further:
            qT[:, lanes(p + 2)] = acc.astype(BF).T
        lse, delta = [], []
        for h in range(2):
            hs = slice(h * E, (h + 1) * E)
            total = out[h][E : E + 1]
            o = out[h][:E] / total
            d = jnp.sum(goT[hs, at].astype(F32) * o, axis=0, keepdims=True)
            mflat[h, :, at] = jnp.broadcast_to(top[h], (8, PAIR))
            if ahead:
                mrow[h] = jnp.broadcast_to(then[h], (8, PAIR))
            both = top[h] + jnp.log2(total)
            lse += [both[:, :128], both[:, 128:]]
            delta += [d[:, :128], d[:, 128:]]
            ob = o.astype(BF)
            for half in range(2):
                obuf[2 * p + half, hs, :] = ob[:, half * 128 : (half + 1) * 128]
        sbuf[p] = jnp.concatenate(lse + delta, axis=0)
        for k in range(1, N_SEQ):
            stat_copy(p, k).start()

    def merge(p):
        wait_bytes(srecv.at[p, pl.ds(1, N_SEQ - 1)], st_r.at[p])
        everyone = [sbuf[p]] + [srecv[p, k] for k in range(1, N_SEQ)]
        top = functools.reduce(jnp.maximum, [e[0:4] for e in everyone])
        factors = [jnp.exp2(e[0:4] - top) for e in everyone]
        total = sum(factors)
        delta = sum(e[4:8] * f for e, f in zip(everyone, factors)) / total
        lse = top + jnp.log2(total)
        share = factors[0] / total
        at = slice(p * PAIR, (p + 1) * PAIR)
        for h in range(2):
            hs = slice(h * E, (h + 1) * E)
            rows = [jnp.concatenate([a[2 * h : 2 * h + 1], a[2 * h + 1 : 2 * h + 2]], axis=1) for a in (lse, delta, share)]
            f = jnp.exp2(mflat[h, 0:1, at] - rows[0])
            fflat[h, 0:1, at] = f
            fflat[h, 1:2, at] = rows[1]
            fflat[h, 2:3, at] = rows[2]
            gosT[hs, at] = (goT[hs, at].astype(F32) * f).astype(BF)
            fqT[hs, at] = (qT[hs, at].astype(F32) * f).astype(BF)

    def rows_of(c):
        return pl.ds(*CHUNKS[c])

    def kept(h, c):
        start, size = CHUNKS[c]
        return lat.at[h * N_CHUNK + start // CHUNK, pl.ds(start % CHUNK, size)]

    def grad_scores(h, c):
        hs = slice(h * E, (h + 1) * E)
        rc = rows_of(c)
        if c < 2:
            dp = jnp.concatenate([early[c][h, p * 128 : (p + 1) * 128, :] for p in range(N_PAIR)], axis=1)
        else:
            dp = dot(v_s[rc, hs], goT[hs, :])
        ds = (wT[h, rc, :].astype(F32) * (dp - fflat[h, 1:2, :])).astype(BF)
        kept(h, c)[...] = ds
        dq = dot(kT[hs, rc], ds)
        dqT[hs, :] = dq if c == 0 else dqT[hs, :] + dq

    class Blocks:
        axes = ((on_y, y_ends), (on_z, z_ends))

        def copies(self, h, stage):
            on, ends = self.axes[h ^ stage]
            src, dst = ((tot1, r1), (tot2, r2))[stage]
            n = 2 * h + stage
            return [remote(src.at[h, on[d + 1]], dst.at[h, d], f_s.at[n], f_r.at[n], ends[d]) for d in range(3)]

        def start(self, h, block):
            for b in range(N_SEQ):
                to, row = (b % 4, b // 4) if h == 0 else (b // 4, b % 4)
                tot1[h, to, row * 128 : (row + 1) * 128, :] = block(h, b).astype(BF)
            for copy in self.copies(h, 0):
                copy.start()

        def total(self, h, stage):
            src, dst = ((tot1, r1), (tot2, r2))[stage]
            wait_bytes(dst.at[h], f_r.at[2 * h + stage])
            me = self.axes[h ^ stage][0][0]
            return src[h, me].astype(F32) + sum(dst[h, d].astype(F32) for d in range(3))

        def second(self, h):
            got = self.total(h, 0).astype(BF)
            for j in range(4):
                tot2[h, j] = got[j * 128 : (j + 1) * 128, :]
            for copy in self.copies(h, 1):
                copy.start()

        def finish(self, h):
            return self.total(h, 1)

        def drain(self):
            for h in range(2):
                wait_bytes(r1.at[h], f_s.at[2 * h])
                wait_bytes(r2.at[h], f_s.at[2 * h + 1])

    outs = Blocks()

    def out_block(h, b):
        at = slice(b * 128, (b + 1) * 128)
        return obuf[b, h * E : (h + 1) * E, :].astype(F32) * fflat[h, 2:3, at]

    def send_query(h):
        for b in range(N_SEQ):
            at = slice(b * 128, (b + 1) * 128)
            dqbuf[h, b] = (dqT[h * E : (h + 1) * E, at] * (fflat[h, 0:1, at] * SCALE)).astype(BF)
        for k in range(1, N_SEQ):
            remote(dqbuf.at[h, peer(k)], dqrecv.at[h, k], dq_s.at[h], dq_r.at[h], (peer(k), head)).start()

    def own_query(h):
        wait_bytes(dqrecv.at[h, pl.ds(1, N_SEQ - 1)], dq_r.at[h])
        return dqbuf[h, seq].astype(F32) + sum(dqrecv[h, k].astype(F32) for k in range(1, N_SEQ))

    def grad_keys_values(h, c):
        rc = rows_of(c)
        hs = slice(h * E, (h + 1) * E)
        dkv[rc, hs] = (dot_nt(kept(h, c)[...], fqT[hs, :]) * SCALE).astype(BF)
        dkv[rc, COLS + h * E : COLS + (h + 1) * E] = dot_nt(wT[h, rc, :], gosT[hs, :]).astype(BF)

    def term_of(c):
        start, size = CHUNKS[c]
        return ctxb.at[start // CHUNK, :, :, pl.ds(start % CHUNK, size)]

    def context_term(c):
        rc = rows_of(c)
        for n in range(8):
            term_of(c)[n % 2, n // 2] = dot_nt(dkv[rc, :], wkv[n * COLS : (n + 1) * COLS, :]).astype(BF)
        parts[c].sib_start()

    class Heads:
        def __init__(self, n, term, sib, ring):
            self.n, self.sib, self.total = n, sib, term.at[core]
            self.c_sib = remote(term.at[1 - core], sib, sib_s.at[n // N_PART], sib_r.at[n], sibling)
            self.ring = Ring(n, ring_sems, on_x, x_ends, self.total, *ring)

        def sib_start(self):
            self.c_sib.start()

        def a(self):
            self.c_sib.wait_recv()
            for j in range(4):
                self.total[j] = (self.total[j].astype(F32) + self.sib[j].astype(F32)).astype(BF)
            self.ring.step_a()

        def b(self):
            self.ring.step_b()

        def finish(self):
            return self.ring.finish()

    def part(c):
        start, size = CHUNKS[c]
        block, rc = start // CHUNK, pl.ds(start % CHUNK, size)
        ring = (arecv.at[block, :, pl.ds(start % CHUNK // 2, size // 2)], bsend.at[block, :, rc], brecv.at[block, :, rc])
        return Heads(c, term_of(c), sibrecv.at[block, :, rc], (*ring, size // 2))

    parts = [part(c) for c in range(N_PART)]
    latent_part = Heads(N_PART, ltb, lsib, (larecv, lbsend, lbrecv, 64))

    turn(N_CHUNK - 1)
    for h in range(2):
        m = None
        for j in range(0, TOK, CHUNK):
            m = scores(0, h, j, m)
        mrow[h] = jnp.broadcast_to(m, (8, PAIR))
    pl.semaphore_wait(barrier, N_SEQ - 1 + 4)

    def step(p, _):
        forward(p, True, True)
        return 0

    lax.fori_loop(0, N_PAIR - 2, step, 0)
    forward(N_PAIR - 2, True, False)
    forward(N_PAIR - 1, False, False)
    for p in range(N_PAIR - 1):
        merge(p)
    early = (sc, sc1)
    for c in range(2):
        for h in range(2):
            hs = slice(h * E, (h + 1) * E)
            for p in range(N_PAIR):
                early[c][h, p * 128 : (p + 1) * 128, :] = dot(v_s[rows_of(c), hs], goT[hs, p * PAIR : (p + 1) * PAIR])
    merge(N_PAIR - 1)
    for h in range(2):
        outs.start(h, out_block)

    def both_heads(f, c):
        for h in range(2):
            f(h, c)

    both_heads(grad_scores, 0)
    both_heads(grad_keys_values, 0)
    context_term(0)
    both_heads(grad_scores, 1)
    both_heads(grad_keys_values, 1)
    context_term(1)
    parts[0].a()
    for c in (2, 3, 4):
        grad_scores(0, c)
    send_query(0)
    parts[1].a()
    grad_scores(1, 2)
    grad_keys_values(0, 2)
    parts[0].b()
    grad_keys_values(1, 2)
    context_term(2)
    grad_scores(1, 3)
    grad_scores(1, 4)
    send_query(1)
    grad_keys_values(0, 3)
    parts[1].b()
    parts[2].a()
    grad_keys_values(1, 3)
    context_term(3)
    both_heads(grad_keys_values, 4)
    parts[3].a()
    context_term(4)
    parts[2].b()
    for h in range(2):
        outs.second(h)
    parts[4].a()
    parts[3].b()

    def store_context(c):
        rc = rows_of(c)
        return pltpu.make_async_copy(gc_ref.at[rc], gc_out.at[rc], out_sem.at[c])

    def finish_context(c):
        gc_ref[rows_of(c), :] = parts[c].finish().astype(BF)
        store_context(c).start()

    store_attention = pltpu.make_async_copy(att_ref, att_out, out_sem.at[N_PART])
    store_latents = pltpu.make_async_copy(gl_ref, gl_out, out_sem.at[N_PART + 1])

    dq = jnp.concatenate([own_query(h) for h in range(2)], axis=0).astype(BF).T
    for n in range(8):
        ltb[n % 2, n // 2] = dot_nt(dq, wq[n * COLS : (n + 1) * COLS, :]).astype(BF)
    latent_part.sib_start()

    for h in range(2):
        att_ref[:, h * E : (h + 1) * E] = outs.finish(h).T.astype(BF)
    store_attention.start()
    latent_part.a()
    parts[4].b()
    finish_context(0)
    finish_context(1)
    finish_context(2)
    latent_part.b()
    finish_context(3)
    finish_context(4)
    gl_ref[...] = latent_part.finish().astype(BF)
    store_latents.start()

    wait_bytes(srecv.at[:, pl.ds(1, N_SEQ - 1)], st_s.at[0])
    for h in range(2):
        wait_bytes(dqrecv.at[h, pl.ds(1, N_SEQ - 1)], dq_s.at[h])
    for n, sent in enumerate(((sibrecv, arecv, brecv), (lsib, larecv, lbrecv))):
        for ref, sem in zip(sent, (sib_s, a_s, b_s)):
            wait_bytes(ref, sem.at[n])
    outs.drain()
    for c in range(N_PART):
        store_context(c).wait()
    store_attention.wait()
    store_latents.wait()


def body(latents, context, offsets, w_query, w_key, w_value, grad_out):
    hbm = pl.BlockSpec(memory_space=pltpu.HBM)
    v, dma = pltpu.VMEM, pltpu.SemaphoreType.DMA
    return pl.pallas_call(
        kernel,
        out_shape=(
            jax.ShapeDtypeStruct((LAT // N_SEQ, COLS), BF),
            jax.ShapeDtypeStruct((LAT // N_SEQ, COLS), BF),
            jax.ShapeDtypeStruct((TOK, COLS), BF),
        ),
        in_specs=[hbm] * 7,
        out_specs=(pl.BlockSpec(memory_space=pl.ANY),) * 3,
        scratch_shapes=[
            v((LAT // N_SEQ, COLS), BF),
            v((LAT // N_SEQ, COLS), BF),
            v((TOK, COLS), BF),
            v((N_PAIR, 1, PAIR), jnp.int32),
            v((N_PAIR, PAIR, WIDE), BF),
            v((WIDE, COLS), BF),
            v((WIDE, 2 * COLS), BF),
            v((LAT, COLS), BF),
            v((COLS, LAT), BF),
            v((TOK, COLS), BF),
            v((TOK, COLS), BF),
            v((COLS, TOK), BF),
            v((2, E + 16, TOK), BF),
            v((COLS, LAT), BF),
            v((2, TOK, LAT), BF),
            v((2, TOK, PAIR), F32),
            v((2, TOK, PAIR), F32),
            v((2, 8, PAIR), F32),
            v((2, 8, LAT), F32),
            v((2, 8, LAT), F32),
            v((N_PAIR, 8, 128), F32),
            v((N_PAIR, N_SEQ, 8, 128), F32),
            v((N_SEQ, COLS, 128), BF),
            v((COLS, LAT), BF),
            v((COLS, LAT), BF),
            v((COLS, LAT), F32),
            v((TOK, 2 * COLS), BF),
            v((2, 4, 512, 128), BF),
            v((2, 3, 512, 128), BF),
            v((2, 4, 128, 128), BF),
            v((2, 3, 128, 128), BF),
            v((2, N_SEQ, 128, 128), BF),
            v((2, N_SEQ, 128, 128), BF),
            v((N_CHUNK, 2, 4, CHUNK, COLS), BF),
            v((N_CHUNK, 4, CHUNK, COLS), BF),
            v((N_CHUNK, 2, CHUNK // 2, COLS), BF),
            v((N_CHUNK, 2, CHUNK, COLS), BF),
            v((N_CHUNK, 2, CHUNK, COLS), BF),
            v((2, 4, 128, COLS), BF),
            v((4, 128, COLS), BF),
            v((2, 64, COLS), BF),
            v((2, 128, COLS), BF),
            v((2, 128, COLS), BF),
            dma((20,)),
            dma((1,)),
            dma((N_PAIR,)),
            *[dma((4,))] * 2,
            *[dma((2,))] * 2,
            dma((2,)),
            dma((N_PART + 1,)),
            *[dma((2,)), dma((N_PART + 1, 2))] * 2,
            dma((N_PART + 2,)),
        ],
        compiler_params=pltpu.CompilerParams(
            collective_id=0, has_side_effects=True, vmem_limit_bytes=52 * 1024 * 1024
        ),
        cost_estimate=pl.CostEstimate(flops=13_000_000_000, bytes_accessed=20_000_000, transcendentals=4_200_000),
    )(
        *[
            pltpu.with_memory_space_constraint(a, pltpu.HBM)
            for a in (latents, context, offsets.reshape(N_PAIR, 1, PAIR), w_query, w_key, w_value, grad_out)
        ]
    )


def solution(mesh):
    placed = (
        P(),
        P("seq", None),
        P(),
        P(None, "head"),
        P(None, "head"),
        P(None, "head"),
        P(None, "head"),
    )
    return jax.shard_map(
        body,
        mesh=mesh,
        in_specs=placed,
        out_specs=(P("seq", "head"), P("seq", "head"), P("seq", "head")),
        check_vma=False,
    )
```
